32 devices in a mesh: section: 2 (over x), expert: 16 (over z, y, core).
Axes of the slice: x: 2, y: 2, z: 4, core: 2. Of those that a mesh axis runs over, the one named last changes fastest.
Arguments:
- grad_out: bfloat16 [2, 3072, 2048], P('section', 'expert'), may hold values from -6 to 6
- layer_input: bfloat16 [2, 3072, 2048], P('section', 'expert'), may hold values from -6 to 6
- routes: int32 [2, 3072, 8], P('section', 'expert'), may hold values from 0 to 63, as said below
- route_logits: float32 [2, 3072, 8], P('section', 'expert'), may hold values from -6 to 6
- gate_weight: bfloat16 [2, 16, 2048, 768], P('section', 'expert'), may hold values from -0.125 to 0.125
- up_weight: bfloat16 [2, 16, 2048, 768], P('section', 'expert'), may hold values from -0.125 to 0.125
- down_weight: bfloat16 [2, 16, 768, 2048], P('section', 'expert'), may hold values from -0.21875 to 0.21875
- router_weight: bfloat16 [2, 2048, 64], P('section'), may hold values from -0.125 to 0.125
Outputs:
- grad_in: bfloat16 [2, 3072, 2048], P('section', 'expert')
- route_logit_grad: float32 [2, 3072, 8], P('section', 'expert')
The draws below stay inside these ranges and needn't reach their ends.
Inputs may be any that keep to these rules, and one draw needn't show every extreme that they name: `routes`: each token names 8 different experts. Among the tokens of one device no expert is named more than 48 times, and in every section one expert below 16 is named exactly 48 times by the tokens of every device of that section.
All inputs are finite; a program needn't handle non-finite values.
Results may differ from the reference program's by a relative error of at most 0.004.
Values may be sent and summed in bfloat16 or wider, within the bound.
A program may use at most 128 MiB of HBM per device.

```python
import jax
import jax.numpy as jnp
from jax import lax

D = 2048
FF = 768
TOP = 8
T_DEV = 192
TOKENS = 3072
EXPERTS = 16
EXP_ALL = 64
CAP = 48
N_SECTION = 2
N_EXPERT = 16


def routes_block(key, hottest):
    mean_load = T_DEV * TOP // EXP_ALL
    subkeys = jax.random.split(key, 4)
    ranking = jax.random.permutation(subkeys[0], EXP_ALL).astype(jnp.int32)
    where_hot = jnp.argmax(ranking == hottest)
    ranking = ranking.at[where_hot].set(ranking[0]).at[0].set(hottest)
    offsets = jax.random.randint(subkeys[1], (EXP_ALL // 2,), 0, mean_load + 1).astype(jnp.int32)
    offsets = offsets.at[0].set(mean_load)
    loads = jnp.stack([mean_load + offsets, mean_load - offsets], axis=1).reshape(EXP_ALL)
    boundaries = jnp.cumsum(loads).astype(jnp.int32)
    positions = jnp.arange(T_DEV * TOP, dtype=jnp.int32)
    rank_of = jnp.sum((boundaries[None, :] <= positions[:, None]).astype(jnp.int32), axis=1)
    assigned = ranking[rank_of].reshape(TOP, T_DEV).T
    row_order = jax.random.permutation(subkeys[2], T_DEV)
    assigned = assigned[row_order]
    scores = jax.random.randint(subkeys[3], (T_DEV, TOP), 0, 1 << 20).astype(jnp.int32) * TOP + jnp.arange(TOP, dtype=jnp.int32)[None, :]
    assigned = jnp.take_along_axis(assigned, jnp.argsort(scores, axis=1), axis=1)
    return assigned.astype(jnp.int32)


def draw_routes(key, part):
    hottest = jax.random.randint(jax.random.fold_in(key, 7), (N_SECTION,), 0, EXPERTS).astype(jnp.int32)
    block_keys = jax.random.split(jax.random.fold_in(key, 11), N_SECTION * N_EXPERT)
    section_hot = jnp.repeat(hottest, N_EXPERT)
    blocks = jax.vmap(routes_block)(block_keys, section_hot)
    return blocks.reshape(N_SECTION, N_EXPERT * T_DEV, TOP)


def block_levels(rng, extent, pieces, low, top_value):
    loudness = 1.0
    for axis_at, blocks in pieces:
        heights = jax.random.uniform(jax.random.fold_in(jax.random.fold_in(rng, 6), axis_at), (blocks,), jnp.float32, low / len(pieces), top_value / len(pieces))
        loudness = loudness * jnp.repeat(jnp.exp(heights), extent[axis_at] // blocks).reshape((-1,) + (1,) * (len(extent) - 1 - axis_at))
    return loudness


def gaussian(rng, extent, scale, bound, cuts=(), kind=jnp.bfloat16):
    values = scale * jax.random.normal(rng, extent, jnp.float32)
    if cuts:
        values = values * block_levels(rng, extent, cuts, -0.22, 0.18)
    return jnp.clip(values, -bound, bound).astype(kind)


def setup_inputs(seed: int = 0) -> dict:
    seeds = jax.random.split(jax.random.key(seed), 9)
    grad_out = gaussian(seeds[0], (N_SECTION, TOKENS, D), 1.0, 6.0, ((0, 2), (1, 16)))
    layer_input = gaussian(seeds[1], (N_SECTION, TOKENS, D), 1.0, 6.0, ((0, 2), (1, 16)))
    routes = draw_routes(jax.random.fold_in(seeds[8], 71), 0)
    route_logits = gaussian(seeds[3], (N_SECTION, TOKENS, TOP), 1.5, 6.0, ((0, 2), (1, 16)), jnp.float32)
    gate_weight = gaussian(seeds[4], (N_SECTION, EXPERTS, D, FF), D ** -0.5, 0.125, ((0, 2), (1, 16)))
    up_weight = gaussian(seeds[5], (N_SECTION, EXPERTS, D, FF), D ** -0.5, 0.125, ((0, 2), (1, 16)))
    down_weight = gaussian(seeds[6], (N_SECTION, EXPERTS, FF, D), FF ** -0.5, 0.21875, ((0, 2), (1, 16)))
    router_weight = gaussian(seeds[7], (N_SECTION, D, EXP_ALL), D ** -0.5, 0.125, ((0, 2),))
    return dict(grad_out=grad_out, layer_input=layer_input, routes=routes, route_logits=route_logits, gate_weight=gate_weight, up_weight=up_weight, down_weight=down_weight, router_weight=router_weight)


def expert_rows(inputs, grad_rows, w_gate, w_up, w_down):
    pre_gate = jnp.dot(inputs, w_gate, preferred_element_type=jnp.float32)
    pre_up = jnp.dot(inputs, w_up, preferred_element_type=jnp.float32)
    hidden_grad = jnp.dot(grad_rows, w_down.T, preferred_element_type=jnp.float32)
    sigmoid_gate = jax.nn.sigmoid(pre_gate)
    activation = pre_gate * sigmoid_gate
    weight_grad = jnp.sum(hidden_grad * activation * pre_up, axis=-1).astype(jnp.bfloat16)
    gate_grad = (hidden_grad * pre_up * sigmoid_gate * (1.0 + pre_gate * (1.0 - sigmoid_gate))).astype(jnp.bfloat16)
    up_grad = (hidden_grad * activation).astype(jnp.bfloat16)
    pair_grad = jnp.dot(gate_grad, w_gate.T, preferred_element_type=jnp.float32) + jnp.dot(up_grad, w_up.T, preferred_element_type=jnp.float32)
    return pair_grad.astype(jnp.bfloat16), weight_grad


def section_back(operands):
    incoming, inputs, picks, logits, w_gates, w_ups, w_downs, w_router = operands
    token_count = inputs.shape[0]
    top_count = picks.shape[1]
    flat_routes = picks.reshape(-1).astype(jnp.int32)
    route_count = flat_routes.shape[0]
    exponent = jnp.exp(logits)
    route_weight = exponent / jnp.sum(exponent, axis=1, keepdims=True)
    onehot = (flat_routes[:, None] == jnp.arange(EXPERTS, dtype=jnp.int32)[None, :]).astype(jnp.int32)
    rank_inside = jnp.sum((jnp.cumsum(onehot, axis=0) - 1) * onehot, axis=1).astype(jnp.int32)
    width_all = N_EXPERT * CAP
    slot_index = jnp.where(flat_routes < EXPERTS, flat_routes * width_all + rank_inside, EXPERTS * width_all).astype(jnp.int32)
    slot_owner = jnp.full((EXPERTS * width_all + 1,), route_count, jnp.int32)
    slot_owner = slot_owner.at[slot_index].set(jnp.arange(route_count, dtype=jnp.int32))
    slot_owner = slot_owner[: EXPERTS * width_all].reshape(EXPERTS, width_all)
    padded_in = jnp.concatenate([inputs, jnp.zeros((1, D), inputs.dtype)], axis=0)
    padded_grad = jnp.concatenate([incoming, jnp.zeros((1, D), incoming.dtype)], axis=0)
    flat_weight = jnp.concatenate([route_weight.reshape(-1), jnp.zeros((1,), jnp.float32)], axis=0)

    def per_expert(carry, operand):
        expert_sum, weight_flat = carry
        row_ids, w_gate, w_up, w_down = operand
        token_index = jnp.where(row_ids < route_count, row_ids // top_count, token_count).astype(jnp.int32)
        pair_grad, weight_grad = expert_rows(padded_in[token_index], padded_grad[token_index], w_gate, w_up, w_down)
        pair_weight = flat_weight[row_ids]
        expert_sum = expert_sum.at[token_index].add(pair_weight[:, None] * pair_grad.astype(jnp.float32))
        weight_flat = weight_flat.at[row_ids].add(weight_grad.astype(jnp.float32))
        return (expert_sum, weight_flat), None

    initial = (jnp.zeros((token_count + 1, D), jnp.float32), jnp.zeros((route_count + 1,), jnp.float32))
    (expert_sum, weight_flat), unused = lax.scan(per_expert, initial, (slot_owner, w_gates, w_ups, w_downs))
    weight_grad = weight_flat[:route_count].reshape(token_count, top_count)
    center = jnp.sum(route_weight * weight_grad, axis=1, keepdims=True)
    logit_grad = route_weight * (weight_grad - center)
    dense_grad = jnp.zeros((token_count, EXP_ALL), jnp.float32)
    dense_grad = dense_grad.at[jnp.arange(token_count, dtype=jnp.int32)[:, None], picks.astype(jnp.int32)].add(logit_grad)
    router_grad = jnp.dot(dense_grad, w_router.astype(jnp.float32).T, precision=lax.Precision.HIGHEST)
    grad_in = (incoming.astype(jnp.float32) + expert_sum[:token_count] + router_grad).astype(jnp.bfloat16)
    return grad_in, logit_grad


def reference(grad_out, layer_input, routes, route_logits, gate_weight, up_weight, down_weight, router_weight):
    incoming = jnp.roll(grad_out, -1, axis=0)
    grad_in, logit_grad = lax.map(section_back, (incoming, layer_input, routes, route_logits, gate_weight, up_weight, down_weight, router_weight))
    return grad_in, logit_grad
```

```python
import functools

import jax
import jax.numpy as jnp
from jax import lax
from jax.experimental import pallas as pl
from jax.experimental.pallas import tpu as pltpu
from jax.sharding import PartitionSpec as P

MESH = pl.DeviceIdType.MESH
LINE = 4
LANES = 128
F32 = jnp.float32
BF16 = jnp.bfloat16


def dot_nt(a, b):
    return lax.dot_general(a, b, (((1,), (1,)), ((), ())), preferred_element_type=F32)


def dot_tn(a, b):
    return lax.dot_general(a, b, (((0,), (0,)), ((), ())), preferred_element_type=F32)


def kernel(
    sections, experts, cap,
    x_ref, grad_ref, routes_ref, logits_ref, gate_ref, up_ref, down_ref,
    total_ref, dots_ref,
    both, pack, rows, ret, back, part, fold, fold_in, meta, w_gate, w_up, w_down,
    x_local, w_sem, own_send, line_send, line_recv, meta_send, meta_recv,
    pack_send, pack_recv, ret_send, ret_recv, fold_send, fold_recv, perm_sem,
):
    group = experts // LINE
    tokens, width = both.shape[2], both.shape[3]
    top = routes_ref.shape[0]
    section = lax.axis_index("section")
    me = lax.axis_index("expert")
    p = me // group
    q = me % group
    far = LINE - 1 - p
    before = (section + sections - 1) % sections
    after = (section + 1) % sections

    def at(line, slot):
        return (section, line * group + slot)

    barrier = pltpu.get_barrier_semaphore()
    for step in range(1, LINE):
        pl.semaphore_signal(barrier, inc=1, device_id=at((p + step) % LINE, q), device_id_type=MESH)
    for step in range(1, group):
        pl.semaphore_signal(barrier, inc=1, device_id=at(p, (q + step) % group), device_id_type=MESH)
    for other in (before, after):
        pl.semaphore_signal(barrier, inc=1, device_id=(other, me), device_id_type=MESH)
    weights = [
        pltpu.make_async_copy(src, dst, w_sem.at[n])
        for n, (src, dst) in enumerate(((gate_ref, w_gate), (up_ref, w_up), (down_ref, w_down)))
    ]
    keep_x = pltpu.make_async_copy(x_ref, both.at[0, p], x_local)
    keep_x.start()
    pl.semaphore_wait(barrier, LINE + group)

    def own_x(way):
        return pltpu.make_async_remote_copy(
            src_ref=x_ref, dst_ref=both.at[0, p], send_sem=own_send.at[way],
            recv_sem=line_recv.at[0, p], device_id=at((p + (1, LINE - 1)[way]) % LINE, q),
            device_id_type=MESH,
        )

    def line_copy(kind, origin, way):
        return pltpu.make_async_remote_copy(
            src_ref=both.at[kind, origin], dst_ref=both.at[kind, origin],
            send_sem=line_send.at[kind, origin, way], recv_sem=line_recv.at[kind, origin],
            device_id=at((p + (1, LINE - 1)[way]) % LINE, q), device_id_type=MESH,
        )

    def has(way):
        return (p < LINE - 1) if way == 0 else (p > 0)

    for way in range(2):
        @pl.when(has(way))
        def _():
            own_x(way).start()
    permute = pltpu.make_async_remote_copy(
        src_ref=grad_ref, dst_ref=both.at[1, p], send_sem=perm_sem.at[0], recv_sem=perm_sem.at[1],
        device_id=(before, me), device_id_type=MESH,
    )
    permute.start()

    routes = routes_ref[...]
    exponent = jnp.exp(logits_ref[...])
    share = exponent / jnp.sum(exponent, axis=0, keepdims=True)
    expert_at = lax.broadcasted_iota(jnp.int32, (experts, tokens), 0)
    named = jnp.zeros((experts, tokens), F32)
    weight = jnp.zeros((experts, tokens), F32)
    for k in range(top):
        hit = routes[k:k + 1, :] == expert_at
        named = named + jnp.where(hit, 1.0, 0.0)
        weight = weight + jnp.where(hit, share[k:k + 1, :], 0.0)
    earlier = (
        lax.broadcasted_iota(jnp.int32, (tokens, tokens), 0)
        < lax.broadcasted_iota(jnp.int32, (tokens, tokens), 1)
    )
    rank = jnp.dot(
        named.astype(BF16), jnp.where(earlier, 1.0, 0.0).astype(BF16), preferred_element_type=F32
    )
    meta[p, 0] = jnp.where(named > 0.5, rank, -1.0)
    meta[p, 1] = weight

    def meta_copy(step):
        return pltpu.make_async_remote_copy(
            src_ref=meta.at[p], dst_ref=meta.at[p], send_sem=meta_send.at[step],
            recv_sem=meta_recv.at[step], device_id=at((p + step) % LINE, q), device_id_type=MESH,
        )

    def meta_wait(step):
        slot = (p + LINE - step) % LINE
        return pltpu.make_async_remote_copy(
            src_ref=meta.at[slot], dst_ref=meta.at[slot], send_sem=meta_send.at[step],
            recv_sem=meta_recv.at[step], device_id=at((p + step) % LINE, q), device_id_type=MESH,
        )

    for step in range(1, LINE):
        meta_copy(step).start()
    for copy in weights:
        copy.start()

    def chosen(origin, what, slot):
        table = meta[origin, what]
        return jnp.sum(jnp.where(expert_at == p * group + slot, table, 0.0), axis=0, keepdims=True)

    place = lax.broadcasted_iota(jnp.int32, (cap, tokens), 0).astype(F32)

    def pack_copy(kind, origin, step):
        return pltpu.make_async_remote_copy(
            src_ref=pack.at[kind, origin, step - 1],
            dst_ref=rows.at[kind, origin, q],
            send_sem=pack_send.at[kind, origin, step],
            recv_sem=pack_recv.at[kind, origin, step],
            device_id=at(p, (q + step) % group), device_id_type=MESH,
        )

    def pack_wait(kind, origin, step):
        return pltpu.make_async_remote_copy(
            src_ref=pack.at[kind, origin, step - 1],
            dst_ref=rows.at[kind, origin, (q + group - step) % group],
            send_sem=pack_send.at[kind, origin, step],
            recv_sem=pack_recv.at[kind, origin, step],
            device_id=at(p, (q + step) % group), device_id_type=MESH,
        )

    def do_pack(kind, origin):
        source = both[kind, origin]
        for step in list(range(1, group)) + [0]:
            pick = jnp.where(chosen(origin, 0, (q + step) % group) == place, 1.0, 0.0).astype(BF16)
            packed = jnp.dot(pick, source, preferred_element_type=F32).astype(BF16)
            if step == 0:
                rows[kind, origin, q] = packed
            else:
                pack[kind, origin, step - 1] = packed
                pack_copy(kind, origin, step).start()

    def ret_copy(origin, step):
        slot = (q + group - step) % group
        return pltpu.make_async_remote_copy(
            src_ref=ret.at[origin, slot], dst_ref=back.at[origin, q],
            send_sem=ret_send.at[origin, step], recv_sem=ret_recv.at[origin, step],
            device_id=at(p, slot), device_id_type=MESH,
        )

    def ret_wait(origin, step):
        return pltpu.make_async_remote_copy(
            src_ref=ret.at[origin, (q + group - step) % group],
            dst_ref=back.at[origin, (q + step) % group],
            send_sem=ret_send.at[origin, step], recv_sem=ret_recv.at[origin, step],
            device_id=at(p, (q + group - step) % group), device_id_type=MESH,
        )

    def do_expert(origin):
        for kind in range(2):
            for step in range(1, group):
                pack_wait(kind, origin, step).wait_recv()
        inputs = rows[0, origin].reshape(group * cap, width)
        grads = rows[1, origin].reshape(group * cap, width)
        pre_gate = jnp.dot(inputs, w_gate[...], preferred_element_type=F32)
        pre_up = jnp.dot(inputs, w_up[...], preferred_element_type=F32)
        hidden = dot_nt(grads, w_down[...])
        sigmoid = jax.nn.sigmoid(pre_gate)
        active = pre_gate * sigmoid
        up_grad = hidden * active
        dots = jnp.sum(up_grad * pre_up, axis=1, keepdims=True)
        gate_grad = hidden * pre_up * sigmoid * (1.0 + pre_gate * (1.0 - sigmoid))
        pair = dot_nt(gate_grad.astype(BF16), w_gate[...]) + dot_nt(up_grad.astype(BF16), w_up[...])
        lane = lax.broadcasted_iota(jnp.int32, (group * cap, LANES), 1)
        ret[origin, :, :, :width] = pair.astype(BF16).reshape(group, cap, width)
        ret[origin, :, :, width:] = (
            jnp.where(lane == me, dots, 0.0).astype(BF16).reshape(group, cap, LANES)
        )
        for step in range(1, group):
            ret_copy(origin, step).start()
        back[origin, q] = ret[origin, q]

    def fold_copy(origin, way):
        target = p + 1 - 2 * way
        if way == 0:
            slot = jnp.where(origin == target, LINE, origin)
        else:
            slot = origin
        return pltpu.make_async_remote_copy(
            src_ref=fold.at[origin], dst_ref=fold_in.at[slot],
            send_sem=fold_send.at[origin], recv_sem=fold_recv.at[slot],
            device_id=at((p + (1, LINE - 1)[way]) % LINE, q), device_id_type=MESH,
        )

    def fold_wait(slot):
        return pltpu.make_async_remote_copy(
            src_ref=fold.at[0], dst_ref=fold_in.at[slot],
            send_sem=fold_send.at[0], recv_sem=fold_recv.at[slot],
            device_id=at((p + 1) % LINE, q), device_id_type=MESH,
        )

    def do_combine(origin):
        for step in range(1, group):
            ret_wait(origin, step).wait_recv()
        picks, highs, lows = [], [], []
        for slot in range(group):
            hit = chosen(origin, 0, slot) == place
            weigh = jnp.where(hit, chosen(origin, 1, slot), 0.0)
            high = weigh.astype(BF16)
            picks.append(jnp.where(hit, 1.0, 0.0).astype(BF16))
            highs.append(high)
            lows.append((weigh - high.astype(F32)).astype(BF16))
        pick, high, low = (jnp.concatenate(parts, axis=0) for parts in (picks, highs, lows))
        came = back[origin, :, :, :width].reshape(group * cap, width)
        marks = back[origin, :, :, width:].reshape(group * cap, LANES)
        part[origin, :, :width] = dot_tn(high, came) + dot_tn(low, came)
        part[origin, :, width:] = dot_tn(pick, marks)

        @pl.when((p == LINE - 1) & (origin < p))
        def _():
            fold[origin] = part[origin].astype(BF16)
            fold_copy(origin, 1).start()

        @pl.when((p == 0) & (origin > p))
        def _():
            fold[origin] = part[origin].astype(BF16)
            fold_copy(origin, 0).start()

    keep_x.wait()
    do_pack(0, p)
    for step in range(1, LINE):
        meta_wait(step).wait_recv()
    permute.wait_recv()

    def arrival(way, i):
        count = p if way == 0 else far
        kind = jnp.where(i >= count, 1, 0)
        if way == 0:
            origin = jnp.where(i >= count, i - count, p - 1 - i)
        else:
            origin = jnp.where(i >= count, LINE - 1 - (i - count), p + 1 + i)
        valid = (i >= 0) & (i < 2 * count)
        return valid, kind, jnp.clip(origin, 0, LINE - 1)

    def candidate(n, i):
        valid_up, kind_up, origin_up = arrival(0, i)
        valid_down, kind_down, origin_down = arrival(1, i)
        valid = jnp.where(n == 0, jnp.where(i == 0, 1, 0), jnp.where(
            n == 1, jnp.where(valid_up, 1, 0), jnp.where(valid_down, 1, 0)))
        kind = jnp.where(n == 0, 1, jnp.where(n == 1, kind_up, kind_down))
        origin = jnp.where(n == 0, p, jnp.where(n == 1, origin_up, origin_down))
        return valid == 1, kind, origin

    def turn(i, carry):
        for way in range(2):
            valid, kind, origin = arrival(way, i)

            @pl.when(valid)
            def _():
                line_copy(kind, origin, way).wait_recv()

                @pl.when(has(way))
                def _():
                    line_copy(kind, origin, way).start()

            count = p if way == 0 else far

            @pl.when((i == 2 * count) & has(way))
            def _():
                line_copy(1, p, way).start()

        def each(step, body):
            def one(n, carry):
                valid, kind, origin = candidate(n, step)
                body(valid, kind, origin)
                return carry

            lax.fori_loop(0, 3, one, 0)

        def pack_one(valid, kind, origin):
            @pl.when(valid)
            def _():
                do_pack(kind, origin)

        def combine_one(valid, kind, origin):
            @pl.when(valid & (kind == 1))
            def _():
                do_combine(origin)

        def expert_one(valid, kind, origin):
            @pl.when(valid & (kind == 1))
            def _():
                do_expert(origin)

        each(i, pack_one)
        each(i - 1, combine_one)

        @pl.when(i == 0)
        def _():
            for copy in weights:
                copy.wait()

        each(i, expert_one)
        return carry

    lax.fori_loop(0, 2 * LINE - 1, turn, 0)

    def gather_back(r, carry):
        @pl.when((p < LINE - 1) & (r <= p))
        def _():
            fold_wait(r).wait_recv()
            part[r] = part[r] + fold_in[r].astype(F32)

            @pl.when(r < p)
            def _():
                fold[r] = part[r].astype(BF16)
                fold_copy(r, 1).start()

        origin = LINE - 1 - r

        @pl.when((p > 0) & (origin >= p))
        def _():
            slot = jnp.where(origin == p, LINE, origin)
            fold_wait(slot).wait_recv()
            part[origin] = part[origin] + fold_in[slot].astype(F32)

            @pl.when(origin > p)
            def _():
                fold[origin] = part[origin].astype(BF16)
                fold_copy(origin, 0).start()

        return carry

    lax.fori_loop(0, LINE, gather_back, 0)
    total_ref[...] = part[p, :, :width] + both[1, p].astype(F32)
    dots_ref[...] = part[p, :, width:]

    permute.wait_send()
    for step in range(1, LINE):
        meta_copy(step).wait_send()
    for way in range(2):
        @pl.when(has(way))
        def _():
            own_x(way).wait_send()
            line_copy(1, p, way).wait_send()

    def finish(origin, carry):
        for kind in range(2):
            for step in range(1, group):
                pack_copy(kind, origin, step).wait_send()

            @pl.when((origin < p) & has(0))
            def _():
                line_copy(kind, origin, 0).wait_send()

            @pl.when((origin > p) & has(1))
            def _():
                line_copy(kind, origin, 1).wait_send()

        for step in range(1, group):
            ret_copy(origin, step).wait_send()

        @pl.when(origin < p)
        def _():
            fold_copy(origin, 1).wait_send()

        @pl.when(origin > p)
        def _():
            fold_copy(origin, 0).wait_send()

        return carry

    lax.fori_loop(0, LINE, finish, 0)


def exchange(sections, x, grad, routes, logits, w_gate, w_up, w_down, capacity):
    tokens, width = x.shape
    hidden = w_gate.shape[1]
    experts = lax.axis_size("expert")
    group = experts // LINE
    cap = -(-capacity // 16) * 16
    wide = width + LANES
    vmem = pl.BlockSpec(memory_space=pltpu.VMEM)
    anywhere = pl.BlockSpec(memory_space=pl.ANY)
    dma = pltpu.SemaphoreType.DMA
    flops = 2 * LINE * group * cap * width * hidden * 5
    return pl.pallas_call(
        functools.partial(kernel, sections, experts, cap),
        out_shape=(
            jax.ShapeDtypeStruct((tokens, width), F32),
            jax.ShapeDtypeStruct((tokens, LANES), F32),
        ),
        in_specs=[anywhere, anywhere, vmem, vmem, anywhere, anywhere, anywhere],
        out_specs=(vmem, vmem),
        scratch_shapes=[
            pltpu.VMEM((2, LINE, tokens, width), BF16),
            pltpu.VMEM((2, LINE, group - 1, cap, width), BF16),
            pltpu.VMEM((2, LINE, group, cap, width), BF16),
            pltpu.VMEM((LINE, group, cap, wide), BF16),
            pltpu.VMEM((LINE, group, cap, wide), BF16),
            pltpu.VMEM((LINE, tokens, wide), F32),
            pltpu.VMEM((LINE, tokens, wide), BF16),
            pltpu.VMEM((LINE + 1, tokens, wide), BF16),
            pltpu.VMEM((LINE, 2, experts, tokens), F32),
            pltpu.VMEM((width, hidden), BF16),
            pltpu.VMEM((width, hidden), BF16),
            pltpu.VMEM((hidden, width), BF16),
            dma(()),
            dma((3,)),
            dma((2,)),
            dma((2, LINE, 2)),
            dma((2, LINE)),
            dma((LINE,)),
            dma((LINE,)),
            dma((2, LINE, group)),
            dma((2, LINE, group)),
            dma((LINE, group)),
            dma((LINE, group)),
            dma((LINE,)),
            dma((LINE + 1,)),
            dma((2,)),
        ],
        compiler_params=pltpu.CompilerParams(
            collective_id=0, has_side_effects=True, vmem_limit_bytes=63 * 1024 * 1024
        ),
        cost_estimate=pl.CostEstimate(
            flops=flops, bytes_accessed=2 * 3 * width * hidden, transcendentals=0
        ),
    )(x, grad, routes, logits, w_gate, w_up, w_down)


def per_device(
    grad_out, layer_input, routes, route_logits, gate_weight, up_weight, down_weight, router_weight
):
    token_count = layer_input.shape[1]
    top_count = routes.shape[2]
    every_expert = router_weight.shape[2]
    capacity = 2 * token_count * top_count // every_expert
    w_router = router_weight[0]
    picks = routes[0]
    total, dots = exchange(
        lax.axis_size("section"), layer_input[0], grad_out[0], picks.T, route_logits[0].T,
        gate_weight[0, 0], up_weight[0, 0], down_weight[0, 0], capacity,
    )
    exponent = jnp.exp(route_logits[0])
    route_weight = exponent / jnp.sum(exponent, axis=1, keepdims=True)
    lane = jnp.arange(LANES, dtype=jnp.int32)[None, None, :]
    weight_grad = jnp.sum(jnp.where(picks[:, :, None] == lane, dots[:, None, :], 0.0), axis=2)
    center = jnp.sum(route_weight * weight_grad, axis=1, keepdims=True)
    logit_grad = route_weight * (weight_grad - center)
    matches = picks[:, :, None] == jnp.arange(every_expert, dtype=jnp.int32)[None, None, :]
    dense_grad = jnp.sum(jnp.where(matches, logit_grad[:, :, None], 0.0), axis=1)
    router_grad = jnp.dot(
        dense_grad, w_router.astype(jnp.float32).T, precision=lax.Precision.HIGHEST
    )
    grad_in = (total + router_grad).astype(jnp.bfloat16)
    return (grad_in[None], logit_grad[None])


def solution(mesh):
    in_specs = (
        P("section", "expert", None),
        P("section", "expert", None),
        P("section", "expert", None),
        P("section", "expert", None),
        P("section", "expert", None, None),
        P("section", "expert", None, None),
        P("section", "expert", None, None),
        P("section", None, None),
    )
    out_specs = (P("section", "expert", None), P("section", "expert", None))
    return jax.shard_map(
        per_device, mesh=mesh, in_specs=in_specs, out_specs=out_specs, check_vma=False
    )
```

```python
import functools

import jax
import jax.numpy as jnp
from jax import lax
from jax.experimental import pallas as pl
from jax.experimental.pallas import tpu as pltpu
from jax.sharding import PartitionSpec as P

MESH = pl.DeviceIdType.MESH
LINE = 4
LANES = 128
F32 = jnp.float32
BF16 = jnp.bfloat16


def dot_nt(a, b):
    return lax.dot_general(a, b, (((1,), (1,)), ((), ())), preferred_element_type=F32)


def dot_tn(a, b):
    return lax.dot_general(a, b, (((0,), (0,)), ((), ())), preferred_element_type=F32)


def kernel(
    sections, experts, cap,
    x_ref, grad_ref, routes_ref, logits_ref, gate_ref, up_ref, down_ref,
    total_ref, dots_ref,
    both, pack, rows, ret, back, part, fold, fold_in, meta, gate_act, up_act, w_gate, w_up, w_down,
    x_local, w_sem, own_send, line_send, line_recv, meta_send, meta_recv,
    pack_send, pack_recv, ret_send, ret_recv, fold_send, fold_recv, perm_sem,
):
    group = experts // LINE
    tokens, width = both.shape[2], both.shape[3]
    top = routes_ref.shape[0]
    section = lax.axis_index("section")
    me = lax.axis_index("expert")
    p = me // group
    q = me % group
    far = LINE - 1 - p
    before = (section + sections - 1) % sections
    after = (section + 1) % sections

    def at(line, slot):
        return (section, line * group + slot)

    barrier = pltpu.get_barrier_semaphore()
    for step in range(1, LINE):
        pl.semaphore_signal(barrier, inc=1, device_id=at((p + step) % LINE, q), device_id_type=MESH)
    for step in range(1, group):
        pl.semaphore_signal(barrier, inc=1, device_id=at(p, (q + step) % group), device_id_type=MESH)
    for other in (before, after):
        pl.semaphore_signal(barrier, inc=1, device_id=(other, me), device_id_type=MESH)
    weights = [
        pltpu.make_async_copy(src, dst, w_sem.at[n])
        for n, (src, dst) in enumerate(((gate_ref, w_gate), (up_ref, w_up), (down_ref, w_down)))
    ]
    keep_x = pltpu.make_async_copy(x_ref, both.at[0, p], x_local)
    keep_x.start()
    pl.semaphore_wait(barrier, LINE + group)

    def own_x(way):
        return pltpu.make_async_remote_copy(
            src_ref=x_ref, dst_ref=both.at[0, p], send_sem=own_send.at[way],
            recv_sem=line_recv.at[0, p], device_id=at((p + (1, LINE - 1)[way]) % LINE, q),
            device_id_type=MESH,
        )

    def line_copy(kind, origin, way):
        return pltpu.make_async_remote_copy(
            src_ref=both.at[kind, origin], dst_ref=both.at[kind, origin],
            send_sem=line_send.at[kind, origin, way], recv_sem=line_recv.at[kind, origin],
            device_id=at((p + (1, LINE - 1)[way]) % LINE, q), device_id_type=MESH,
        )

    def has(way):
        return (p < LINE - 1) if way == 0 else (p > 0)

    for way in range(2):
        @pl.when(has(way))
        def _():
            own_x(way).start()
    permute = pltpu.make_async_remote_copy(
        src_ref=grad_ref, dst_ref=both.at[1, p], send_sem=perm_sem.at[0], recv_sem=perm_sem.at[1],
        device_id=(before, me), device_id_type=MESH,
    )
    permute.start()

    routes = routes_ref[...]
    exponent = jnp.exp(logits_ref[...])
    share = exponent / jnp.sum(exponent, axis=0, keepdims=True)
    expert_at = lax.broadcasted_iota(jnp.int32, (experts, tokens), 0)
    named = jnp.zeros((experts, tokens), F32)
    weight = jnp.zeros((experts, tokens), F32)
    for k in range(top):
        hit = routes[k:k + 1, :] == expert_at
        named = named + jnp.where(hit, 1.0, 0.0)
        weight = weight + jnp.where(hit, share[k:k + 1, :], 0.0)
    earlier = (
        lax.broadcasted_iota(jnp.int32, (tokens, tokens), 0)
        < lax.broadcasted_iota(jnp.int32, (tokens, tokens), 1)
    )
    rank = jnp.dot(
        named.astype(BF16), jnp.where(earlier, 1.0, 0.0).astype(BF16), preferred_element_type=F32
    )
    meta[p, 0] = jnp.where(named > 0.5, rank, -1.0)
    meta[p, 1] = weight

    def meta_copy(step):
        return pltpu.make_async_remote_copy(
            src_ref=meta.at[p], dst_ref=meta.at[p], send_sem=meta_send.at[step],
            recv_sem=meta_recv.at[step], device_id=at((p + step) % LINE, q), device_id_type=MESH,
        )

    def meta_wait(step):
        slot = (p + LINE - step) % LINE
        return pltpu.make_async_remote_copy(
            src_ref=meta.at[slot], dst_ref=meta.at[slot], send_sem=meta_send.at[step],
            recv_sem=meta_recv.at[step], device_id=at((p + step) % LINE, q), device_id_type=MESH,
        )

    for step in range(1, LINE):
        meta_copy(step).start()
    for copy in weights:
        copy.start()

    def chosen(origin, what, slot):
        table = meta[origin, what]
        return jnp.sum(jnp.where(expert_at == p * group + slot, table, 0.0), axis=0, keepdims=True)

    place = lax.broadcasted_iota(jnp.int32, (cap, tokens), 0).astype(F32)

    def pack_copy(kind, origin, step):
        return pltpu.make_async_remote_copy(
            src_ref=pack.at[kind, origin, step - 1],
            dst_ref=rows.at[kind, origin, q],
            send_sem=pack_send.at[kind, origin, step],
            recv_sem=pack_recv.at[kind, origin, step],
            device_id=at(p, (q + step) % group), device_id_type=MESH,
        )

    def pack_wait(kind, origin, step):
        return pltpu.make_async_remote_copy(
            src_ref=pack.at[kind, origin, step - 1],
            dst_ref=rows.at[kind, origin, (q + group - step) % group],
            send_sem=pack_send.at[kind, origin, step],
            recv_sem=pack_recv.at[kind, origin, step],
            device_id=at(p, (q + step) % group), device_id_type=MESH,
        )

    def do_pack(kind, origin):
        source = both[kind, origin]
        for step in list(range(1, group)) + [0]:
            pick = jnp.where(chosen(origin, 0, (q + step) % group) == place, 1.0, 0.0).astype(BF16)
            packed = jnp.dot(pick, source, preferred_element_type=F32).astype(BF16)
            if step == 0:
                rows[kind, origin, q] = packed
            else:
                pack[kind, origin, step - 1] = packed
                pack_copy(kind, origin, step).start()

    def ret_copy(origin, step):
        slot = (q + group - step) % group
        return pltpu.make_async_remote_copy(
            src_ref=ret.at[origin, slot], dst_ref=back.at[origin, q],
            send_sem=ret_send.at[origin, step], recv_sem=ret_recv.at[origin, step],
            device_id=at(p, slot), device_id_type=MESH,
        )

    def ret_wait(origin, step):
        return pltpu.make_async_remote_copy(
            src_ref=ret.at[origin, (q + group - step) % group],
            dst_ref=back.at[origin, (q + step) % group],
            send_sem=ret_send.at[origin, step], recv_sem=ret_recv.at[origin, step],
            device_id=at(p, (q + group - step) % group), device_id_type=MESH,
        )

    def do_front(origin):
        for step in range(1, group):
            pack_wait(0, origin, step).wait_recv()
        inputs = rows[0, origin].reshape(group * cap, width)
        gate_act[origin] = jnp.dot(inputs, w_gate[...], preferred_element_type=F32)
        up_act[origin] = jnp.dot(inputs, w_up[...], preferred_element_type=F32)

    def do_back(origin):
        for step in range(1, group):
            pack_wait(1, origin, step).wait_recv()
        grads = rows[1, origin].reshape(group * cap, width)
        hidden = dot_nt(grads, w_down[...])
        pre_gate = gate_act[origin]
        pre_up = up_act[origin]
        sigmoid = jax.nn.sigmoid(pre_gate)
        active = pre_gate * sigmoid
        up_grad = hidden * active
        dots = jnp.sum(up_grad * pre_up, axis=1, keepdims=True)
        gate_grad = hidden * pre_up * sigmoid * (1.0 + pre_gate * (1.0 - sigmoid))
        pair = dot_nt(gate_grad.astype(BF16), w_gate[...]) + dot_nt(up_grad.astype(BF16), w_up[...])
        lane = lax.broadcasted_iota(jnp.int32, (group * cap, LANES), 1)
        ret[origin, :, :, :width] = pair.astype(BF16).reshape(group, cap, width)
        ret[origin, :, :, width:] = (
            jnp.where(lane == me, dots, 0.0).astype(BF16).reshape(group, cap, LANES)
        )
        for step in range(1, group):
            ret_copy(origin, step).start()
        back[origin, q] = ret[origin, q]

    def fold_copy(origin, way):
        target = p + 1 - 2 * way
        if way == 0:
            slot = jnp.where(origin == target, LINE, origin)
        else:
            slot = origin
        return pltpu.make_async_remote_copy(
            src_ref=fold.at[origin], dst_ref=fold_in.at[slot],
            send_sem=fold_send.at[origin], recv_sem=fold_recv.at[slot],
            device_id=at((p + (1, LINE - 1)[way]) % LINE, q), device_id_type=MESH,
        )

    def fold_wait(slot):
        return pltpu.make_async_remote_copy(
            src_ref=fold.at[0], dst_ref=fold_in.at[slot],
            send_sem=fold_send.at[0], recv_sem=fold_recv.at[slot],
            device_id=at((p + 1) % LINE, q), device_id_type=MESH,
        )

    def do_combine(origin):
        for step in range(1, group):
            ret_wait(origin, step).wait_recv()
        picks, highs, lows = [], [], []
        for slot in range(group):
            hit = chosen(origin, 0, slot) == place
            weigh = jnp.where(hit, chosen(origin, 1, slot), 0.0)
            high = weigh.astype(BF16)
            picks.append(jnp.where(hit, 1.0, 0.0).astype(BF16))
            highs.append(high)
            lows.append((weigh - high.astype(F32)).astype(BF16))
        pick, high, low = (jnp.concatenate(parts, axis=0) for parts in (picks, highs, lows))
        came = back[origin, :, :, :width].reshape(group * cap, width)
        marks = back[origin, :, :, width:].reshape(group * cap, LANES)
        part[origin, :, :width] = dot_tn(high, came) + dot_tn(low, came)
        part[origin, :, width:] = dot_tn(pick, marks)

        @pl.when((p == LINE - 1) & (origin < p))
        def _():
            fold[origin] = part[origin].astype(BF16)
            fold_copy(origin, 1).start()

        @pl.when((p == 0) & (origin > p))
        def _():
            fold[origin] = part[origin].astype(BF16)
            fold_copy(origin, 0).start()

    keep_x.wait()
    do_pack(0, p)
    for step in range(1, LINE):
        meta_wait(step).wait_recv()
    permute.wait_recv()

    def arrival(way, i):
        count = p if way == 0 else far
        kind = jnp.where(i >= count, 1, 0)
        if way == 0:
            origin = jnp.where(i >= count, i - count, p - 1 - i)
        else:
            origin = jnp.where(i >= count, LINE - 1 - (i - count), p + 1 + i)
        valid = (i >= 0) & (i < 2 * count)
        return valid, kind, jnp.clip(origin, 0, LINE - 1)

    def candidate(n, i):
        valid_up, kind_up, origin_up = arrival(0, i)
        valid_down, kind_down, origin_down = arrival(1, i)
        own = (i == 0) | (i == -1)
        valid = jnp.where(n == 0, jnp.where(own, 1, 0), jnp.where(
            n == 1, jnp.where(valid_up, 1, 0), jnp.where(valid_down, 1, 0)))
        kind = jnp.where(n == 0, i + 1, jnp.where(n == 1, kind_up, kind_down))
        origin = jnp.where(n == 0, p, jnp.where(n == 1, origin_up, origin_down))
        return valid == 1, kind, origin

    late = jnp.where((p == 0) | (p == LINE - 1), 0, 1)

    def turn(i, carry):
        for way in range(2):
            valid, kind, origin = arrival(way, i)

            @pl.when(valid)
            def _():
                line_copy(kind, origin, way).wait_recv()

                @pl.when(has(way))
                def _():
                    line_copy(kind, origin, way).start()

            count = p if way == 0 else far

            @pl.when((i == 2 * count) & has(way))
            def _():
                line_copy(1, p, way).start()

        def each(step, body):
            def one(n, carry):
                valid, kind, origin = candidate(n, step)
                body(valid, kind, origin)
                return carry

            lax.fori_loop(0, 3, one, 0)

        def pack_one(valid, kind, origin):
            @pl.when(valid)
            def _():
                do_pack(kind, origin)

        def combine_one(valid, kind, origin):
            @pl.when(valid & (kind == 1))
            def _():
                do_combine(origin)

        def front_one(valid, kind, origin):
            @pl.when(valid & (kind == 0))
            def _():
                do_front(origin)

        def back_one(valid, kind, origin):
            @pl.when(valid & (kind == 1))
            def _():
                do_back(origin)

        each(i, pack_one)

        @pl.when(i == 0)
        def _():
            for copy in weights:
                copy.wait()

        each(i - 1, front_one)

        @pl.when(late == 0)
        def _():
            each(i - 1, combine_one)

        each(i - late, back_one)

        @pl.when(late == 1)
        def _():
            each(i - 2, combine_one)

        return carry

    lax.fori_loop(0, 2 * LINE - 1, turn, 0)

    def gather_back(r, carry):
        @pl.when((p < LINE - 1) & (r <= p))
        def _():
            fold_wait(r).wait_recv()
            part[r] = part[r] + fold_in[r].astype(F32)

            @pl.when(r < p)
            def _():
                fold[r] = part[r].astype(BF16)
                fold_copy(r, 1).start()

        origin = LINE - 1 - r

        @pl.when((p > 0) & (origin >= p))
        def _():
            slot = jnp.where(origin == p, LINE, origin)
            fold_wait(slot).wait_recv()
            part[origin] = part[origin] + fold_in[slot].astype(F32)

            @pl.when(origin > p)
            def _():
                fold[origin] = part[origin].astype(BF16)
                fold_copy(origin, 0).start()

        return carry

    lax.fori_loop(0, LINE, gather_back, 0)
    total_ref[...] = part[p, :, :width] + both[1, p].astype(F32)
    dots_ref[...] = part[p, :, width:]

    permute.wait_send()
    for step in range(1, LINE):
        meta_copy(step).wait_send()
    for way in range(2):
        @pl.when(has(way))
        def _():
            own_x(way).wait_send()
            line_copy(1, p, way).wait_send()

    def finish(origin, carry):
        for kind in range(2):
            for step in range(1, group):
                pack_copy(kind, origin, step).wait_send()

            @pl.when((origin < p) & has(0))
            def _():
                line_copy(kind, origin, 0).wait_send()

            @pl.when((origin > p) & has(1))
            def _():
                line_copy(kind, origin, 1).wait_send()

        for step in range(1, group):
            ret_copy(origin, step).wait_send()

        @pl.when(origin < p)
        def _():
            fold_copy(origin, 1).wait_send()

        @pl.when(origin > p)
        def _():
            fold_copy(origin, 0).wait_send()

        return carry

    lax.fori_loop(0, LINE, finish, 0)


def exchange(sections, x, grad, routes, logits, w_gate, w_up, w_down, capacity):
    tokens, width = x.shape
    hidden = w_gate.shape[1]
    experts = lax.axis_size("expert")
    group = experts // LINE
    cap = -(-capacity // 16) * 16
    wide = width + LANES
    vmem = pl.BlockSpec(memory_space=pltpu.VMEM)
    anywhere = pl.BlockSpec(memory_space=pl.ANY)
    dma = pltpu.SemaphoreType.DMA
    flops = 2 * LINE * group * cap * width * hidden * 5
    return pl.pallas_call(
        functools.partial(kernel, sections, experts, cap),
        out_shape=(
            jax.ShapeDtypeStruct((tokens, width), F32),
            jax.ShapeDtypeStruct((tokens, LANES), F32),
        ),
        in_specs=[anywhere, anywhere, vmem, vmem, anywhere, anywhere, anywhere],
        out_specs=(vmem, vmem),
        scratch_shapes=[
            pltpu.VMEM((2, LINE, tokens, width), BF16),
            pltpu.VMEM((2, LINE, group - 1, cap, width), BF16),
            pltpu.VMEM((2, LINE, group, cap, width), BF16),
            pltpu.VMEM((LINE, group, cap, wide), BF16),
            pltpu.VMEM((LINE, group, cap, wide), BF16),
            pltpu.VMEM((LINE, tokens, wide), F32),
            pltpu.VMEM((LINE, tokens, wide), BF16),
            pltpu.VMEM((LINE + 1, tokens, wide), BF16),
            pltpu.VMEM((LINE, 2, experts, tokens), F32),
            pltpu.VMEM((LINE, group * cap, hidden), F32),
            pltpu.VMEM((LINE, group * cap, hidden), F32),
            pltpu.VMEM((width, hidden), BF16),
            pltpu.VMEM((width, hidden), BF16),
            pltpu.VMEM((hidden, width), BF16),
            dma(()),
            dma((3,)),
            dma((2,)),
            dma((2, LINE, 2)),
            dma((2, LINE)),
            dma((LINE,)),
            dma((LINE,)),
            dma((2, LINE, group)),
            dma((2, LINE, group)),
            dma((LINE, group)),
            dma((LINE, group)),
            dma((LINE,)),
            dma((LINE + 1,)),
            dma((2,)),
        ],
        compiler_params=pltpu.CompilerParams(
            collective_id=0, has_side_effects=True, vmem_limit_bytes=63 * 1024 * 1024
        ),
        cost_estimate=pl.CostEstimate(
            flops=flops, bytes_accessed=2 * 3 * width * hidden, transcendentals=0
        ),
    )(x, grad, routes, logits, w_gate, w_up, w_down)


def per_device(
    grad_out, layer_input, routes, route_logits, gate_weight, up_weight, down_weight, router_weight
):
    token_count = layer_input.shape[1]
    top_count = routes.shape[2]
    every_expert = router_weight.shape[2]
    capacity = 2 * token_count * top_count // every_expert
    w_router = router_weight[0]
    picks = routes[0]
    total, dots = exchange(
        lax.axis_size("section"), layer_input[0], grad_out[0], picks.T, route_logits[0].T,
        gate_weight[0, 0], up_weight[0, 0], down_weight[0, 0], capacity,
    )
    exponent = jnp.exp(route_logits[0])
    route_weight = exponent / jnp.sum(exponent, axis=1, keepdims=True)
    lane = jnp.arange(LANES, dtype=jnp.int32)[None, None, :]
    weight_grad = jnp.sum(jnp.where(picks[:, :, None] == lane, dots[:, None, :], 0.0), axis=2)
    center = jnp.sum(route_weight * weight_grad, axis=1, keepdims=True)
    logit_grad = route_weight * (weight_grad - center)
    matches = picks[:, :, None] == jnp.arange(every_expert, dtype=jnp.int32)[None, None, :]
    dense_grad = jnp.sum(jnp.where(matches, logit_grad[:, :, None], 0.0), axis=1)
    router_grad = jnp.dot(
        dense_grad, w_router.astype(jnp.float32).T, precision=lax.Precision.HIGHEST
    )
    grad_in = (total + router_grad).astype(jnp.bfloat16)
    return (grad_in[None], logit_grad[None])


def solution(mesh):
    in_specs = (
        P("section", "expert", None),
        P("section", "expert", None),
        P("section", "expert", None),
        P("section", "expert", None),
        P("section", "expert", None, None),
        P("section", "expert", None, None),
        P("section", "expert", None, None),
        P("section", None, None),
    )
    out_specs = (P("section", "expert", None), P("section", "expert", None))
    return jax.shard_map(
        per_device, mesh=mesh, in_specs=in_specs, out_specs=out_specs, check_vma=False
    )
```

```python
import functools

import jax
import jax.numpy as jnp
from jax import lax
from jax.experimental import pallas as pl
from jax.experimental.pallas import tpu as pltpu
from jax.sharding import PartitionSpec as P

MESH = pl.DeviceIdType.MESH
LINE = 4
LANES = 128
PIECES = 2
F32 = jnp.float32
BF16 = jnp.bfloat16


def dot_nt(a, b):
    return lax.dot_general(a, b, (((1,), (1,)), ((), ())), preferred_element_type=F32)


def dot_tn(a, b):
    return lax.dot_general(a, b, (((0,), (0,)), ((), ())), preferred_element_type=F32)


def kernel(
    sections, experts, cap,
    x_ref, grad_ref, routes_ref, logits_ref, gate_ref, up_ref, down_ref,
    total_ref, dots_ref,
    both, pack, rows, ret, back, part, fold, fold_in, meta, gate_act, up_act, w_gate, w_up, w_down,
    x_local, w_sem, own_send, line_send, line_recv, meta_send, meta_recv,
    pack_send, pack_recv, ret_send, ret_recv, fold_send, fold_recv, perm_sem,
):
    group = experts // LINE
    tokens, width = both.shape[2], both.shape[3]
    top = routes_ref.shape[0]
    section = lax.axis_index("section")
    me = lax.axis_index("expert")
    p = me // group
    q = me % group
    far = LINE - 1 - p
    part_width = width // PIECES

    def cut(piece):
        return pl.ds(piece * part_width, part_width)

    def cut_wide(piece):
        return pl.ds(piece * part_width, part_width + (LANES if piece == PIECES - 1 else 0))

    before = (section + sections - 1) % sections
    after = (section + 1) % sections

    def at(line, slot):
        return (section, line * group + slot)

    barrier = pltpu.get_barrier_semaphore()
    for step in range(1, LINE):
        pl.semaphore_signal(barrier, inc=1, device_id=at((p + step) % LINE, q), device_id_type=MESH)
    for step in range(1, group):
        pl.semaphore_signal(barrier, inc=1, device_id=at(p, (q + step) % group), device_id_type=MESH)
    for other in (before, after):
        pl.semaphore_signal(barrier, inc=1, device_id=(other, me), device_id_type=MESH)
    weights = [
        pltpu.make_async_copy(src, dst, w_sem.at[n])
        for n, (src, dst) in enumerate(((gate_ref, w_gate), (up_ref, w_up), (down_ref, w_down)))
    ]
    keep_x = pltpu.make_async_copy(x_ref, both.at[0, p], x_local)
    keep_x.start()
    pl.semaphore_wait(barrier, LINE + group)

    def own_x(way, piece):
        return pltpu.make_async_remote_copy(
            src_ref=x_ref.at[:, cut(piece)], dst_ref=both.at[0, p, :, cut(piece)],
            send_sem=own_send.at[way, piece],
            recv_sem=line_recv.at[0, p, piece], device_id=at((p + (1, LINE - 1)[way]) % LINE, q),
            device_id_type=MESH,
        )

    def line_copy(kind, origin, way, piece):
        return pltpu.make_async_remote_copy(
            src_ref=both.at[kind, origin, :, cut(piece)],
            dst_ref=both.at[kind, origin, :, cut(piece)],
            send_sem=line_send.at[kind, origin, way, piece],
            recv_sem=line_recv.at[kind, origin, piece],
            device_id=at((p + (1, LINE - 1)[way]) % LINE, q), device_id_type=MESH,
        )

    def has(way):
        return (p < LINE - 1) if way == 0 else (p > 0)

    def permute(piece):
        return pltpu.make_async_remote_copy(
            src_ref=grad_ref.at[:, cut(piece)], dst_ref=both.at[1, p, :, cut(piece)],
            send_sem=perm_sem.at[0, piece], recv_sem=perm_sem.at[1, piece],
            device_id=(before, me), device_id_type=MESH,
        )

    for piece in range(PIECES):
        for way in range(2):
            @pl.when(has(way))
            def _():
                own_x(way, piece).start()
        permute(piece).start()

    routes = routes_ref[...]
    exponent = jnp.exp(logits_ref[...])
    share = exponent / jnp.sum(exponent, axis=0, keepdims=True)
    expert_at = lax.broadcasted_iota(jnp.int32, (experts, tokens), 0)
    named = jnp.zeros((experts, tokens), F32)
    weight = jnp.zeros((experts, tokens), F32)
    for k in range(top):
        hit = routes[k:k + 1, :] == expert_at
        named = named + jnp.where(hit, 1.0, 0.0)
        weight = weight + jnp.where(hit, share[k:k + 1, :], 0.0)
    earlier = (
        lax.broadcasted_iota(jnp.int32, (tokens, tokens), 0)
        < lax.broadcasted_iota(jnp.int32, (tokens, tokens), 1)
    )
    rank = jnp.dot(
        named.astype(BF16), jnp.where(earlier, 1.0, 0.0).astype(BF16), preferred_element_type=F32
    )
    meta[p, 0] = jnp.where(named > 0.5, rank, -1.0)
    meta[p, 1] = weight

    def meta_copy(step):
        return pltpu.make_async_remote_copy(
            src_ref=meta.at[p], dst_ref=meta.at[p], send_sem=meta_send.at[step],
            recv_sem=meta_recv.at[step], device_id=at((p + step) % LINE, q), device_id_type=MESH,
        )

    def meta_wait(step):
        slot = (p + LINE - step) % LINE
        return pltpu.make_async_remote_copy(
            src_ref=meta.at[slot], dst_ref=meta.at[slot], send_sem=meta_send.at[step],
            recv_sem=meta_recv.at[step], device_id=at((p + step) % LINE, q), device_id_type=MESH,
        )

    for step in range(1, LINE):
        meta_copy(step).start()
    for copy in weights:
        copy.start()

    def chosen(origin, what, slot):
        table = meta[origin, what]
        return jnp.sum(jnp.where(expert_at == p * group + slot, table, 0.0), axis=0, keepdims=True)

    place = lax.broadcasted_iota(jnp.int32, (cap, tokens), 0).astype(F32)

    def pack_copy(kind, origin, step, piece):
        return pltpu.make_async_remote_copy(
            src_ref=pack.at[kind, origin, step - 1, :, cut(piece)],
            dst_ref=rows.at[kind, origin, q, :, cut(piece)],
            send_sem=pack_send.at[kind, origin, step, piece],
            recv_sem=pack_recv.at[kind, origin, step, piece],
            device_id=at(p, (q + step) % group), device_id_type=MESH,
        )

    def pack_wait(kind, origin, step, piece):
        return pltpu.make_async_remote_copy(
            src_ref=pack.at[kind, origin, step - 1, :, cut(piece)],
            dst_ref=rows.at[kind, origin, (q + group - step) % group, :, cut(piece)],
            send_sem=pack_send.at[kind, origin, step, piece],
            recv_sem=pack_recv.at[kind, origin, step, piece],
            device_id=at(p, (q + step) % group), device_id_type=MESH,
        )

    def do_pack(kind, origin, piece):
        source = both[kind, origin, :, cut(piece)]
        for step in list(range(1, group)) + [0]:
            pick = jnp.where(chosen(origin, 0, (q + step) % group) == place, 1.0, 0.0).astype(BF16)
            packed = jnp.dot(pick, source, preferred_element_type=F32).astype(BF16)
            if step == 0:
                rows[kind, origin, q, :, cut(piece)] = packed
            else:
                pack[kind, origin, step - 1, :, cut(piece)] = packed
                pack_copy(kind, origin, step, piece).start()

    def ret_copy(origin, step, piece):
        slot = (q + group - step) % group
        return pltpu.make_async_remote_copy(
            src_ref=ret.at[origin, slot, :, cut_wide(piece)],
            dst_ref=back.at[origin, q, :, cut_wide(piece)],
            send_sem=ret_send.at[origin, step, piece], recv_sem=ret_recv.at[origin, step, piece],
            device_id=at(p, slot), device_id_type=MESH,
        )

    def ret_wait(origin, step, piece):
        return pltpu.make_async_remote_copy(
            src_ref=ret.at[origin, (q + group - step) % group, :, cut_wide(piece)],
            dst_ref=back.at[origin, (q + step) % group, :, cut_wide(piece)],
            send_sem=ret_send.at[origin, step, piece], recv_sem=ret_recv.at[origin, step, piece],
            device_id=at(p, (q + group - step) % group), device_id_type=MESH,
        )

    def do_front(origin):
        for piece in range(PIECES):
            for step in range(1, group):
                pack_wait(0, origin, step, piece).wait_recv()
        inputs = rows[0, origin].reshape(group * cap, width)
        gate_act[origin] = jnp.dot(inputs, w_gate[...], preferred_element_type=F32)
        up_act[origin] = jnp.dot(inputs, w_up[...], preferred_element_type=F32)

    def do_back(origin):
        hidden = jnp.zeros((group * cap, w_down.shape[0]), F32)
        for piece in range(PIECES):
            for step in range(1, group):
                pack_wait(1, origin, step, piece).wait_recv()
            grads = rows[1, origin, :, :, cut(piece)].reshape(group * cap, part_width)
            hidden = hidden + dot_nt(grads, w_down[:, cut(piece)])
        pre_gate = gate_act[origin]
        pre_up = up_act[origin]
        sigmoid = jax.nn.sigmoid(pre_gate)
        active = pre_gate * sigmoid
        up_grad = hidden * active
        dots = jnp.sum(up_grad * pre_up, axis=1, keepdims=True)
        gate_grad = hidden * pre_up * sigmoid * (1.0 + pre_gate * (1.0 - sigmoid))
        gate_grad = gate_grad.astype(BF16)
        up_grad = up_grad.astype(BF16)
        lane = lax.broadcasted_iota(jnp.int32, (group * cap, LANES), 1)
        ret[origin, :, :, width:] = (
            jnp.where(lane == me, dots, 0.0).astype(BF16).reshape(group, cap, LANES)
        )
        for piece in range(PIECES):
            pair = dot_nt(gate_grad, w_gate[cut(piece), :]) + dot_nt(up_grad, w_up[cut(piece), :])
            ret[origin, :, :, cut(piece)] = pair.astype(BF16).reshape(group, cap, part_width)
            for step in range(1, group):
                ret_copy(origin, step, piece).start()
        back[origin, q] = ret[origin, q]

    def fold_copy(origin, way, piece):
        target = p + 1 - 2 * way
        if way == 0:
            slot = jnp.where(origin == target, LINE, origin)
        else:
            slot = origin
        return pltpu.make_async_remote_copy(
            src_ref=fold.at[origin, :, cut_wide(piece)],
            dst_ref=fold_in.at[slot, :, cut_wide(piece)],
            send_sem=fold_send.at[origin, piece], recv_sem=fold_recv.at[slot, piece],
            device_id=at((p + (1, LINE - 1)[way]) % LINE, q), device_id_type=MESH,
        )

    def fold_wait(slot, piece):
        return pltpu.make_async_remote_copy(
            src_ref=fold.at[0, :, cut_wide(piece)], dst_ref=fold_in.at[slot, :, cut_wide(piece)],
            send_sem=fold_send.at[0, piece], recv_sem=fold_recv.at[slot, piece],
            device_id=at((p + 1) % LINE, q), device_id_type=MESH,
        )

    def do_combine(origin):
        picks, highs, lows = [], [], []
        for slot in range(group):
            hit = chosen(origin, 0, slot) == place
            weigh = jnp.where(hit, chosen(origin, 1, slot), 0.0)
            high = weigh.astype(BF16)
            picks.append(jnp.where(hit, 1.0, 0.0).astype(BF16))
            highs.append(high)
            lows.append((weigh - high.astype(F32)).astype(BF16))
        pick, high, low = (jnp.concatenate(parts, axis=0) for parts in (picks, highs, lows))
        for piece in range(PIECES):
            for step in range(1, group):
                ret_wait(origin, step, piece).wait_recv()
            came = back[origin, :, :, cut(piece)].reshape(group * cap, part_width)
            part[origin, :, cut(piece)] = dot_tn(high, came) + dot_tn(low, came)
            if piece == PIECES - 1:
                marks = back[origin, :, :, width:].reshape(group * cap, LANES)
                part[origin, :, width:] = dot_tn(pick, marks)

            @pl.when((p == LINE - 1) & (origin < p))
            def _():
                fold[origin, :, cut_wide(piece)] = part[origin, :, cut_wide(piece)].astype(BF16)
                fold_copy(origin, 1, piece).start()

            @pl.when((p == 0) & (origin > p))
            def _():
                fold[origin, :, cut_wide(piece)] = part[origin, :, cut_wide(piece)].astype(BF16)
                fold_copy(origin, 0, piece).start()

    keep_x.wait()
    for piece in range(PIECES):
        do_pack(0, p, piece)
    for step in range(1, LINE):
        meta_wait(step).wait_recv()

    def arrival(way, i):
        count = p if way == 0 else far
        kind = jnp.where(i >= count, 1, 0)
        if way == 0:
            origin = jnp.where(i >= count, i - count, p - 1 - i)
        else:
            origin = jnp.where(i >= count, LINE - 1 - (i - count), p + 1 + i)
        valid = (i >= 0) & (i < 2 * count)
        return valid, kind, jnp.clip(origin, 0, LINE - 1)

    def candidate(n, i):
        valid_up, kind_up, origin_up = arrival(0, i)
        valid_down, kind_down, origin_down = arrival(1, i)
        own = (i == 0) | (i == -1)
        valid = jnp.where(n == 0, jnp.where(own, 1, 0), jnp.where(
            n == 1, jnp.where(valid_up, 1, 0), jnp.where(valid_down, 1, 0)))
        kind = jnp.where(n == 0, i + 1, jnp.where(n == 1, kind_up, kind_down))
        origin = jnp.where(n == 0, p, jnp.where(n == 1, origin_up, origin_down))
        return valid == 1, kind, origin

    late = jnp.where((p == 0) | (p == LINE - 1), 0, 1)

    def turn(i, carry):
        def forward(piece):
            @pl.when(i == 0)
            def _():
                permute(piece).wait_recv()

            for way in range(2):
                valid, kind, origin = arrival(way, i)

                @pl.when(valid)
                def _():
                    line_copy(kind, origin, way, piece).wait_recv()

                    @pl.when(has(way))
                    def _():
                        line_copy(kind, origin, way, piece).start()

        def own_gradients():
            for way in range(2):
                count = p if way == 0 else far

                @pl.when((i == jnp.maximum(2 * count - 1, 0)) & has(way))
                def _():
                    for piece in range(PIECES):
                        line_copy(1, p, way, piece).start()

        def each(step, body):
            def one(n, carry):
                valid, kind, origin = candidate(n, step)
                body(valid, kind, origin)
                return carry

            lax.fori_loop(0, 3, one, 0)

        def pack_one(piece, valid, kind, origin):
            @pl.when(valid)
            def _():
                do_pack(kind, origin, piece)

        def combine_one(valid, kind, origin):
            @pl.when(valid & (kind == 1))
            def _():
                do_combine(origin)

        def front_one(valid, kind, origin):
            @pl.when(valid & (kind == 0))
            def _():
                do_front(origin)

        def back_one(valid, kind, origin):
            @pl.when(valid & (kind == 1))
            def _():
                do_back(origin)

        for piece in range(PIECES):
            forward(piece)
            if piece == PIECES - 1:
                own_gradients()
            each(i, functools.partial(pack_one, piece))

        @pl.when(i == 0)
        def _():
            for copy in weights:
                copy.wait()

        each(i - 1, front_one)

        @pl.when(late == 0)
        def _():
            each(i - 1, combine_one)

        each(i - late, back_one)

        @pl.when(late == 1)
        def _():
            each(i - 2, combine_one)

        return carry

    lax.fori_loop(0, 2 * LINE - 1, turn, 0)

    def gather_back(r, carry):
        origin = LINE - 1 - r
        slot = jnp.where(origin == p, LINE, origin)
        for piece in range(PIECES):
            where = cut_wide(piece)

            @pl.when((p < LINE - 1) & (r <= p))
            def _():
                fold_wait(r, piece).wait_recv()
                summed = part[r, :, where] + fold_in[r, :, where].astype(F32)

                @pl.when(r < p)
                def _():
                    fold[r, :, where] = summed.astype(BF16)
                    fold_copy(r, 1, piece).start()

                @pl.when(r == p)
                def _():
                    part[r, :, where] = summed

            @pl.when((p > 0) & (origin >= p))
            def _():
                fold_wait(slot, piece).wait_recv()
                summed = part[origin, :, where] + fold_in[slot, :, where].astype(F32)

                @pl.when(origin > p)
                def _():
                    fold[origin, :, where] = summed.astype(BF16)
                    fold_copy(origin, 0, piece).start()

                @pl.when(origin == p)
                def _():
                    part[origin, :, where] = summed

        return carry

    lax.fori_loop(0, LINE, gather_back, 0)
    total_ref[...] = part[p, :, :width] + both[1, p].astype(F32)
    dots_ref[...] = part[p, :, width:]

    for step in range(1, LINE):
        meta_copy(step).wait_send()
    for piece in range(PIECES):
        permute(piece).wait_send()
        for way in range(2):
            @pl.when(has(way))
            def _():
                own_x(way, piece).wait_send()
                line_copy(1, p, way, piece).wait_send()

    def finish(origin, carry):
        for piece in range(PIECES):
            for kind in range(2):
                for step in range(1, group):
                    pack_copy(kind, origin, step, piece).wait_send()

                @pl.when((origin < p) & has(0))
                def _():
                    line_copy(kind, origin, 0, piece).wait_send()

                @pl.when((origin > p) & has(1))
                def _():
                    line_copy(kind, origin, 1, piece).wait_send()

            for step in range(1, group):
                ret_copy(origin, step, piece).wait_send()

            @pl.when(origin < p)
            def _():
                fold_copy(origin, 1, piece).wait_send()

            @pl.when(origin > p)
            def _():
                fold_copy(origin, 0, piece).wait_send()

        return carry

    lax.fori_loop(0, LINE, finish, 0)


def exchange(sections, x, grad, routes, logits, w_gate, w_up, w_down, capacity):
    tokens, width = x.shape
    hidden = w_gate.shape[1]
    experts = lax.axis_size("expert")
    group = experts // LINE
    cap = -(-capacity // 16) * 16
    wide = width + LANES
    vmem = pl.BlockSpec(memory_space=pltpu.VMEM)
    anywhere = pl.BlockSpec(memory_space=pl.ANY)
    dma = pltpu.SemaphoreType.DMA
    flops = 2 * LINE * group * cap * width * hidden * 5
    return pl.pallas_call(
        functools.partial(kernel, sections, experts, cap),
        out_shape=(
            jax.ShapeDtypeStruct((tokens, width), F32),
            jax.ShapeDtypeStruct((tokens, LANES), F32),
        ),
        in_specs=[anywhere, anywhere, vmem, vmem, anywhere, anywhere, anywhere],
        out_specs=(vmem, vmem),
        scratch_shapes=[
            pltpu.VMEM((2, LINE, tokens, width), BF16),
            pltpu.VMEM((2, LINE, group - 1, cap, width), BF16),
            pltpu.VMEM((2, LINE, group, cap, width), BF16),
            pltpu.VMEM((LINE, group, cap, wide), BF16),
            pltpu.VMEM((LINE, group, cap, wide), BF16),
            pltpu.VMEM((LINE, tokens, wide), F32),
            pltpu.VMEM((LINE, tokens, wide), BF16),
            pltpu.VMEM((LINE + 1, tokens, wide), BF16),
            pltpu.VMEM((LINE, 2, experts, tokens), F32),
            pltpu.VMEM((LINE, group * cap, hidden), F32),
            pltpu.VMEM((LINE, group * cap, hidden), F32),
            pltpu.VMEM((width, hidden), BF16),
            pltpu.VMEM((width, hidden), BF16),
            pltpu.VMEM((hidden, width), BF16),
            dma(()),
            dma((3,)),
            dma((2, PIECES)),
            dma((2, LINE, 2, PIECES)),
            dma((2, LINE, PIECES)),
            dma((LINE,)),
            dma((LINE,)),
            dma((2, LINE, group, PIECES)),
            dma((2, LINE, group, PIECES)),
            dma((LINE, group, PIECES)),
            dma((LINE, group, PIECES)),
            dma((LINE, PIECES)),
            dma((LINE + 1, PIECES)),
            dma((2, PIECES)),
        ],
        compiler_params=pltpu.CompilerParams(
            collective_id=0, has_side_effects=True, vmem_limit_bytes=63 * 1024 * 1024
        ),
        cost_estimate=pl.CostEstimate(
            flops=flops, bytes_accessed=2 * 3 * width * hidden, transcendentals=0
        ),
    )(x, grad, routes, logits, w_gate, w_up, w_down)


def per_device(
    grad_out, layer_input, routes, route_logits, gate_weight, up_weight, down_weight, router_weight
):
    token_count = layer_input.shape[1]
    top_count = routes.shape[2]
    every_expert = router_weight.shape[2]
    capacity = 2 * token_count * top_count // every_expert
    w_router = router_weight[0]
    picks = routes[0]
    total, dots = exchange(
        lax.axis_size("section"), layer_input[0], grad_out[0], picks.T, route_logits[0].T,
        gate_weight[0, 0], up_weight[0, 0], down_weight[0, 0], capacity,
    )
    exponent = jnp.exp(route_logits[0])
    route_weight = exponent / jnp.sum(exponent, axis=1, keepdims=True)
    lane = jnp.arange(LANES, dtype=jnp.int32)[None, None, :]
    weight_grad = jnp.sum(jnp.where(picks[:, :, None] == lane, dots[:, None, :], 0.0), axis=2)
    center = jnp.sum(route_weight * weight_grad, axis=1, keepdims=True)
    logit_grad = route_weight * (weight_grad - center)
    matches = picks[:, :, None] == jnp.arange(every_expert, dtype=jnp.int32)[None, None, :]
    dense_grad = jnp.sum(jnp.where(matches, logit_grad[:, :, None], 0.0), axis=1)
    router_grad = jnp.dot(
        dense_grad, w_router.astype(jnp.float32).T, precision=lax.Precision.HIGHEST
    )
    grad_in = (total + router_grad).astype(jnp.bfloat16)
    return (grad_in[None], logit_grad[None])


def solution(mesh):
    in_specs = (
        P("section", "expert", None),
        P("section", "expert", None),
        P("section", "expert", None),
        P("section", "expert", None),
        P("section", "expert", None, None),
        P("section", "expert", None, None),
        P("section", "expert", None, None),
        P("section", None, None),
    )
    out_specs = (P("section", "expert", None), P("section", "expert", None))
    return jax.shard_map(
        per_device, mesh=mesh, in_specs=in_specs, out_specs=out_specs, check_vma=False
    )
```

```python
import functools

import jax
import jax.numpy as jnp
from jax import lax
from jax.experimental import pallas as pl
from jax.experimental.pallas import tpu as pltpu
from jax.sharding import PartitionSpec as P

MESH = pl.DeviceIdType.MESH
LINE = 4
LANES = 128
PIECES = 2
F32 = jnp.float32
BF16 = jnp.bfloat16


def dot_nt(a, b):
    return lax.dot_general(a, b, (((1,), (1,)), ((), ())), preferred_element_type=F32)


def kernel(
    sections, experts, cap,
    x_ref, grad_ref, routes_ref, logits_ref, gate_ref, up_ref, down_ref,
    total_ref, dots_ref,
    both, pack, rows, ret, back, part, fold, fold_in, meta, gate_act, up_act, w_gate, w_up, w_down,
    x_local, w_sem, own_send, line_send, line_recv, meta_send, meta_recv,
    pack_send, pack_recv, ret_send, ret_recv, fold_send, fold_recv, perm_sem,
):
    group = experts // LINE
    tokens, width = both.shape[2], both.shape[3]
    top = routes_ref.shape[0]
    section = lax.axis_index("section")
    me = lax.axis_index("expert")
    p = me // group
    q = me % group
    far = LINE - 1 - p
    part_width = width // PIECES

    def cut(piece):
        return pl.ds(piece * part_width, part_width)

    def cut_wide(piece):
        return pl.ds(piece * part_width, part_width + (LANES if piece == PIECES - 1 else 0))

    before = (section + sections - 1) % sections
    after = (section + 1) % sections

    def at(line, slot):
        return (section, line * group + slot)

    barrier = pltpu.get_barrier_semaphore()
    for step in range(1, LINE):
        pl.semaphore_signal(barrier, inc=1, device_id=at((p + step) % LINE, q), device_id_type=MESH)
    for step in range(1, group):
        pl.semaphore_signal(barrier, inc=1, device_id=at(p, (q + step) % group), device_id_type=MESH)
    for other in (before, after):
        pl.semaphore_signal(barrier, inc=1, device_id=(other, me), device_id_type=MESH)
    weights = [
        pltpu.make_async_copy(src, dst, w_sem.at[n])
        for n, (src, dst) in enumerate(((gate_ref, w_gate), (up_ref, w_up), (down_ref, w_down)))
    ]
    keep_x = pltpu.make_async_copy(x_ref, both.at[0, p], x_local)
    keep_x.start()
    pl.semaphore_wait(barrier, LINE + group)

    def own_x(way, piece):
        return pltpu.make_async_remote_copy(
            src_ref=x_ref.at[:, cut(piece)], dst_ref=both.at[0, p, :, cut(piece)],
            send_sem=own_send.at[way, piece],
            recv_sem=line_recv.at[0, p, piece], device_id=at((p + (1, LINE - 1)[way]) % LINE, q),
            device_id_type=MESH,
        )

    def line_copy(kind, origin, way, piece):
        return pltpu.make_async_remote_copy(
            src_ref=both.at[kind, origin, :, cut(piece)],
            dst_ref=both.at[kind, origin, :, cut(piece)],
            send_sem=line_send.at[kind, origin, way, piece],
            recv_sem=line_recv.at[kind, origin, piece],
            device_id=at((p + (1, LINE - 1)[way]) % LINE, q), device_id_type=MESH,
        )

    def has(way):
        return (p < LINE - 1) if way == 0 else (p > 0)

    def permute(piece):
        return pltpu.make_async_remote_copy(
            src_ref=grad_ref.at[:, cut(piece)], dst_ref=both.at[1, p, :, cut(piece)],
            send_sem=perm_sem.at[0, piece], recv_sem=perm_sem.at[1, piece],
            device_id=(before, me), device_id_type=MESH,
        )

    for piece in range(PIECES):
        for way in range(2):
            @pl.when(has(way))
            def _():
                own_x(way, piece).start()
        permute(piece).start()

    routes = routes_ref[...]
    exponent = jnp.exp(logits_ref[...])
    share = exponent / jnp.sum(exponent, axis=0, keepdims=True)
    expert_at = lax.broadcasted_iota(jnp.int32, (experts, tokens), 0)
    named = jnp.zeros((experts, tokens), F32)
    weight = jnp.zeros((experts, tokens), F32)
    for k in range(top):
        hit = routes[k:k + 1, :] == expert_at
        named = named + jnp.where(hit, 1.0, 0.0)
        weight = weight + jnp.where(hit, share[k:k + 1, :], 0.0)
    earlier = (
        lax.broadcasted_iota(jnp.int32, (tokens, tokens), 0)
        < lax.broadcasted_iota(jnp.int32, (tokens, tokens), 1)
    )
    rank = jnp.dot(
        named.astype(BF16), jnp.where(earlier, 1.0, 0.0).astype(BF16), preferred_element_type=F32
    )
    meta[p, 0] = jnp.where(named > 0.5, rank, -1.0)
    meta[p, 1] = weight

    def meta_copy(step):
        return pltpu.make_async_remote_copy(
            src_ref=meta.at[p], dst_ref=meta.at[p], send_sem=meta_send.at[step],
            recv_sem=meta_recv.at[step], device_id=at((p + step) % LINE, q), device_id_type=MESH,
        )

    def meta_wait(step):
        slot = (p + LINE - step) % LINE
        return pltpu.make_async_remote_copy(
            src_ref=meta.at[slot], dst_ref=meta.at[slot], send_sem=meta_send.at[step],
            recv_sem=meta_recv.at[step], device_id=at((p + step) % LINE, q), device_id_type=MESH,
        )

    for step in range(1, LINE):
        meta_copy(step).start()
    for copy in weights:
        copy.start()

    def chosen(origin, what, slot):
        table = meta[origin, what]
        return jnp.sum(jnp.where(expert_at == p * group + slot, table, 0.0), axis=0, keepdims=True)

    place = lax.broadcasted_iota(jnp.int32, (cap, tokens), 0).astype(F32)

    def pack_copy(kind, origin, step, piece):
        return pltpu.make_async_remote_copy(
            src_ref=pack.at[kind, origin, step - 1, :, cut(piece)],
            dst_ref=rows.at[kind, origin, q, :, cut(piece)],
            send_sem=pack_send.at[kind, origin, step, piece],
            recv_sem=pack_recv.at[kind, origin, step, piece],
            device_id=at(p, (q + step) % group), device_id_type=MESH,
        )

    def pack_wait(kind, origin, step, piece):
        return pltpu.make_async_remote_copy(
            src_ref=pack.at[kind, origin, step - 1, :, cut(piece)],
            dst_ref=rows.at[kind, origin, (q + group - step) % group, :, cut(piece)],
            send_sem=pack_send.at[kind, origin, step, piece],
            recv_sem=pack_recv.at[kind, origin, step, piece],
            device_id=at(p, (q + step) % group), device_id_type=MESH,
        )

    def do_pack(kind, origin, piece):
        source = both[kind, origin, :, cut(piece)]
        for step in list(range(1, group)) + [0]:
            pick = jnp.where(chosen(origin, 0, (q + step) % group) == place, 1.0, 0.0).astype(BF16)
            packed = jnp.dot(pick, source, preferred_element_type=F32).astype(BF16)
            if step == 0:
                rows[kind, origin, q, :, cut(piece)] = packed
            else:
                pack[kind, origin, step - 1, :, cut(piece)] = packed
                pack_copy(kind, origin, step, piece).start()

    def ret_copy(origin, step, piece):
        slot = (q + group - step) % group
        return pltpu.make_async_remote_copy(
            src_ref=ret.at[origin, slot, :, cut_wide(piece)],
            dst_ref=back.at[origin, q, :, cut_wide(piece)],
            send_sem=ret_send.at[origin, step, piece], recv_sem=ret_recv.at[origin, step, piece],
            device_id=at(p, slot), device_id_type=MESH,
        )

    def ret_wait(origin, step, piece):
        return pltpu.make_async_remote_copy(
            src_ref=ret.at[origin, (q + group - step) % group, :, cut_wide(piece)],
            dst_ref=back.at[origin, (q + step) % group, :, cut_wide(piece)],
            send_sem=ret_send.at[origin, step, piece], recv_sem=ret_recv.at[origin, step, piece],
            device_id=at(p, (q + group - step) % group), device_id_type=MESH,
        )

    def do_front(origin):
        for piece in range(PIECES):
            for step in range(1, group):
                pack_wait(0, origin, step, piece).wait_recv()
        inputs = rows[0, origin].reshape(group * cap, width)
        gate_act[origin] = jnp.dot(inputs, w_gate[...], preferred_element_type=F32).T
        up_act[origin] = jnp.dot(inputs, w_up[...], preferred_element_type=F32).T

    def do_back(origin):
        hidden = jnp.zeros((w_down.shape[0], group * cap), F32)
        for piece in range(PIECES):
            for step in range(1, group):
                pack_wait(1, origin, step, piece).wait_recv()
            grads = rows[1, origin, :, :, cut(piece)].reshape(group * cap, part_width)
            hidden = hidden + dot_nt(w_down[:, cut(piece)], grads)
        pre_gate = gate_act[origin]
        pre_up = up_act[origin]
        sigmoid = jax.nn.sigmoid(pre_gate)
        active = pre_gate * sigmoid
        up_grad = hidden * active
        dots = jnp.sum(up_grad * pre_up, axis=0, keepdims=True)
        gate_grad = hidden * pre_up * sigmoid * (1.0 + pre_gate * (1.0 - sigmoid))
        gate_grad = gate_grad.astype(BF16)
        up_grad = up_grad.astype(BF16)
        lane = lax.broadcasted_iota(jnp.int32, (LANES, group * cap), 0)
        ret[origin, :, :, width:] = (
            jnp.where(lane == me, dots, 0.0).T.astype(BF16).reshape(group, cap, LANES)
        )
        for piece in range(PIECES):
            pair = jnp.dot(w_gate[cut(piece), :], gate_grad, preferred_element_type=F32)
            pair = pair + jnp.dot(w_up[cut(piece), :], up_grad, preferred_element_type=F32)
            ret[origin, :, :, cut(piece)] = pair.T.astype(BF16).reshape(group, cap, part_width)
            for step in range(1, group):
                ret_copy(origin, step, piece).start()
        back[origin, q] = ret[origin, q]

    def fold_copy(origin, way, piece):
        target = p + 1 - 2 * way
        if way == 0:
            slot = jnp.where(origin == target, LINE, origin)
        else:
            slot = origin
        return pltpu.make_async_remote_copy(
            src_ref=fold.at[origin, :, cut_wide(piece)],
            dst_ref=fold_in.at[slot, :, cut_wide(piece)],
            send_sem=fold_send.at[origin, piece], recv_sem=fold_recv.at[slot, piece],
            device_id=at((p + (1, LINE - 1)[way]) % LINE, q), device_id_type=MESH,
        )

    def fold_wait(slot, piece):
        return pltpu.make_async_remote_copy(
            src_ref=fold.at[0, :, cut_wide(piece)], dst_ref=fold_in.at[slot, :, cut_wide(piece)],
            send_sem=fold_send.at[0, piece], recv_sem=fold_recv.at[slot, piece],
            device_id=at((p + 1) % LINE, q), device_id_type=MESH,
        )

    def do_combine(origin):
        shares = []
        for slot in range(group):
            hit = chosen(origin, 0, slot) == place
            shares.append(jnp.where(hit, chosen(origin, 1, slot), 0.0))
        weigh = jnp.concatenate(shares, axis=0).T
        high = weigh.astype(BF16)
        low = (weigh - high.astype(F32)).astype(BF16)
        pick = jnp.where(weigh > 0.0, 1.0, 0.0).astype(BF16)
        for piece in range(PIECES):
            for step in range(1, group):
                ret_wait(origin, step, piece).wait_recv()
            came = back[origin, :, :, cut(piece)].reshape(group * cap, part_width)
            part[origin, :, cut(piece)] = (
                jnp.dot(high, came, preferred_element_type=F32)
                + jnp.dot(low, came, preferred_element_type=F32)
            )
            if piece == PIECES - 1:
                marks = back[origin, :, :, width:].reshape(group * cap, LANES)
                part[origin, :, width:] = jnp.dot(pick, marks, preferred_element_type=F32)

            @pl.when((p == LINE - 1) & (origin < p))
            def _():
                fold[origin, :, cut_wide(piece)] = part[origin, :, cut_wide(piece)].astype(BF16)
                fold_copy(origin, 1, piece).start()

            @pl.when((p == 0) & (origin > p))
            def _():
                fold[origin, :, cut_wide(piece)] = part[origin, :, cut_wide(piece)].astype(BF16)
                fold_copy(origin, 0, piece).start()

    keep_x.wait()
    for piece in range(PIECES):
        do_pack(0, p, piece)
    for step in range(1, LINE):
        meta_wait(step).wait_recv()

    def arrival(way, i):
        count = p if way == 0 else far
        kind = jnp.where(i >= count, 1, 0)
        if way == 0:
            origin = jnp.where(i >= count, i - count, p - 1 - i)
        else:
            origin = jnp.where(i >= count, LINE - 1 - (i - count), p + 1 + i)
        valid = (i >= 0) & (i < 2 * count)
        return valid, kind, jnp.clip(origin, 0, LINE - 1)

    def candidate(n, i):
        valid_up, kind_up, origin_up = arrival(0, i)
        valid_down, kind_down, origin_down = arrival(1, i)
        own = (i == 0) | (i == -1)
        valid = jnp.where(n == 0, jnp.where(own, 1, 0), jnp.where(
            n == 1, jnp.where(valid_up, 1, 0), jnp.where(valid_down, 1, 0)))
        kind = jnp.where(n == 0, i + 1, jnp.where(n == 1, kind_up, kind_down))
        origin = jnp.where(n == 0, p, jnp.where(n == 1, origin_up, origin_down))
        return valid == 1, kind, origin

    late = jnp.where((p == 0) | (p == LINE - 1), 0, 1)

    def turn(i, carry):
        def forward(piece):
            @pl.when(i == 0)
            def _():
                permute(piece).wait_recv()

            for way in range(2):
                valid, kind, origin = arrival(way, i)

                @pl.when(valid)
                def _():
                    line_copy(kind, origin, way, piece).wait_recv()

                    @pl.when(has(way))
                    def _():
                        line_copy(kind, origin, way, piece).start()

        def own_gradients():
            for way in range(2):
                count = p if way == 0 else far

                @pl.when((i == jnp.maximum(2 * count - 1, 0)) & has(way))
                def _():
                    for piece in range(PIECES):
                        line_copy(1, p, way, piece).start()

        def each(step, body):
            def one(n, carry):
                valid, kind, origin = candidate(n, step)
                body(valid, kind, origin)
                return carry

            lax.fori_loop(0, 3, one, 0)

        def pack_one(piece, valid, kind, origin):
            @pl.when(valid)
            def _():
                do_pack(kind, origin, piece)

        def combine_one(valid, kind, origin):
            @pl.when(valid & (kind == 1))
            def _():
                do_combine(origin)

        def front_one(valid, kind, origin):
            @pl.when(valid & (kind == 0))
            def _():
                do_front(origin)

        def back_one(valid, kind, origin):
            @pl.when(valid & (kind == 1))
            def _():
                do_back(origin)

        for piece in range(PIECES):
            forward(piece)
            if piece == PIECES - 1:
                own_gradients()
            each(i, functools.partial(pack_one, piece))

        @pl.when(i == 0)
        def _():
            for copy in weights:
                copy.wait()

        each(i - 1, front_one)

        @pl.when(late == 0)
        def _():
            each(i - 1, combine_one)

        each(i - late, back_one)

        @pl.when(late == 1)
        def _():
            each(i - 2, combine_one)

        return carry

    lax.fori_loop(0, 2 * LINE - 1, turn, 0)

    def gather_back(r, carry):
        origin = LINE - 1 - r
        for piece in range(PIECES):
            where = cut_wide(piece)

            @pl.when((p < LINE - 1) & (r < p))
            def _():
                fold_wait(r, piece).wait_recv()
                summed = part[r, :, where] + fold_in[r, :, where].astype(F32)
                fold[r, :, where] = summed.astype(BF16)
                fold_copy(r, 1, piece).start()

            @pl.when((p > 0) & (origin > p))
            def _():
                fold_wait(origin, piece).wait_recv()
                summed = part[origin, :, where] + fold_in[origin, :, where].astype(F32)
                fold[origin, :, where] = summed.astype(BF16)
                fold_copy(origin, 0, piece).start()

        return carry

    lax.fori_loop(0, LINE - 1, gather_back, 0)
    for piece in range(PIECES):
        where = cut_wide(piece)
        for way in range(2):
            @pl.when(has(1 - way))
            def _():
                slot = LINE if way == 0 else p
                fold_wait(slot, piece).wait_recv()
                part[p, :, where] = part[p, :, where] + fold_in[slot, :, where].astype(F32)

    total_ref[...] = part[p, :, :width] + both[1, p].astype(F32)
    dots_ref[...] = part[p, :, width:]

    for step in range(1, LINE):
        meta_copy(step).wait_send()
    for piece in range(PIECES):
        permute(piece).wait_send()
        for way in range(2):
            @pl.when(has(way))
            def _():
                own_x(way, piece).wait_send()
                line_copy(1, p, way, piece).wait_send()

    def finish(origin, carry):
        for piece in range(PIECES):
            for kind in range(2):
                for step in range(1, group):
                    pack_copy(kind, origin, step, piece).wait_send()

                @pl.when((origin < p) & has(0))
                def _():
                    line_copy(kind, origin, 0, piece).wait_send()

                @pl.when((origin > p) & has(1))
                def _():
                    line_copy(kind, origin, 1, piece).wait_send()

            for step in range(1, group):
                ret_copy(origin, step, piece).wait_send()

            @pl.when(origin < p)
            def _():
                fold_copy(origin, 1, piece).wait_send()

            @pl.when(origin > p)
            def _():
                fold_copy(origin, 0, piece).wait_send()

        return carry

    lax.fori_loop(0, LINE, finish, 0)


def exchange(sections, x, grad, routes, logits, w_gate, w_up, w_down, capacity):
    tokens, width = x.shape
    hidden = w_gate.shape[1]
    experts = lax.axis_size("expert")
    group = experts // LINE
    cap = -(-capacity // 16) * 16
    wide = width + LANES
    vmem = pl.BlockSpec(memory_space=pltpu.VMEM)
    anywhere = pl.BlockSpec(memory_space=pl.ANY)
    dma = pltpu.SemaphoreType.DMA
    flops = 2 * LINE * group * cap * width * hidden * 5
    return pl.pallas_call(
        functools.partial(kernel, sections, experts, cap),
        out_shape=(
            jax.ShapeDtypeStruct((tokens, width), F32),
            jax.ShapeDtypeStruct((tokens, LANES), F32),
        ),
        in_specs=[anywhere, anywhere, vmem, vmem, anywhere, anywhere, anywhere],
        out_specs=(vmem, vmem),
        scratch_shapes=[
            pltpu.VMEM((2, LINE, tokens, width), BF16),
            pltpu.VMEM((2, LINE, group - 1, cap, width), BF16),
            pltpu.VMEM((2, LINE, group, cap, width), BF16),
            pltpu.VMEM((LINE, group, cap, wide), BF16),
            pltpu.VMEM((LINE, group, cap, wide), BF16),
            pltpu.VMEM((LINE, tokens, wide), F32),
            pltpu.VMEM((LINE, tokens, wide), BF16),
            pltpu.VMEM((LINE + 1, tokens, wide), BF16),
            pltpu.VMEM((LINE, 2, experts, tokens), F32),
            pltpu.VMEM((LINE, hidden, group * cap), F32),
            pltpu.VMEM((LINE, hidden, group * cap), F32),
            pltpu.VMEM((width, hidden), BF16),
            pltpu.VMEM((width, hidden), BF16),
            pltpu.VMEM((hidden, width), BF16),
            dma(()),
            dma((3,)),
            dma((2, PIECES)),
            dma((2, LINE, 2, PIECES)),
            dma((2, LINE, PIECES)),
            dma((LINE,)),
            dma((LINE,)),
            dma((2, LINE, group, PIECES)),
            dma((2, LINE, group, PIECES)),
            dma((LINE, group, PIECES)),
            dma((LINE, group, PIECES)),
            dma((LINE, PIECES)),
            dma((LINE + 1, PIECES)),
            dma((2, PIECES)),
        ],
        compiler_params=pltpu.CompilerParams(
            collective_id=0, has_side_effects=True, vmem_limit_bytes=63 * 1024 * 1024
        ),
        cost_estimate=pl.CostEstimate(
            flops=flops, bytes_accessed=2 * 3 * width * hidden, transcendentals=0
        ),
    )(x, grad, routes, logits, w_gate, w_up, w_down)


def per_device(
    grad_out, layer_input, routes, route_logits, gate_weight, up_weight, down_weight, router_weight
):
    token_count = layer_input.shape[1]
    top_count = routes.shape[2]
    every_expert = router_weight.shape[2]
    capacity = 2 * token_count * top_count // every_expert
    w_router = router_weight[0]
    picks = routes[0]
    total, dots = exchange(
        lax.axis_size("section"), layer_input[0], grad_out[0], picks.T, route_logits[0].T,
        gate_weight[0, 0], up_weight[0, 0], down_weight[0, 0], capacity,
    )
    exponent = jnp.exp(route_logits[0])
    route_weight = exponent / jnp.sum(exponent, axis=1, keepdims=True)
    lane = jnp.arange(LANES, dtype=jnp.int32)[None, None, :]
    weight_grad = jnp.sum(jnp.where(picks[:, :, None] == lane, dots[:, None, :], 0.0), axis=2)
    center = jnp.sum(route_weight * weight_grad, axis=1, keepdims=True)
    logit_grad = route_weight * (weight_grad - center)
    matches = picks[:, :, None] == jnp.arange(every_expert, dtype=jnp.int32)[None, None, :]
    dense_grad = jnp.sum(jnp.where(matches, logit_grad[:, :, None], 0.0), axis=1)
    router_grad = jnp.dot(
        dense_grad, w_router.astype(jnp.float32).T, precision=lax.Precision.HIGHEST
    )
    grad_in = (total + router_grad).astype(jnp.bfloat16)
    return (grad_in[None], logit_grad[None])


def solution(mesh):
    in_specs = (
        P("section", "expert", None),
        P("section", "expert", None),
        P("section", "expert", None),
        P("section", "expert", None),
        P("section", "expert", None, None),
        P("section", "expert", None, None),
        P("section", "expert", None, None),
        P("section", None, None),
    )
    out_specs = (P("section", "expert", None), P("section", "expert", None))
    return jax.shard_map(
        per_device, mesh=mesh, in_specs=in_specs, out_specs=out_specs, check_vma=False
    )
```

```python
import functools

import jax
import jax.numpy as jnp
from jax import lax
from jax.experimental import pallas as pl
from jax.experimental.pallas import tpu as pltpu
from jax.sharding import PartitionSpec as P

MESH = pl.DeviceIdType.MESH
LINE = 4
LANES = 128
PIECES = 2
F32 = jnp.float32
BF16 = jnp.bfloat16


def dot_nt(a, b):
    return lax.dot_general(a, b, (((1,), (1,)), ((), ())), preferred_element_type=F32)


def kernel(
    sections, experts, cap,
    x_ref, grad_ref, routes_ref, logits_ref, gate_ref, up_ref, down_ref,
    total_ref, dots_ref,
    both, pack, rows, ret, back, part, fold, fold_in, meta, gate_act, up_act, w_gate, w_up, w_down,
    x_local, w_sem, own_send, line_send, line_recv, meta_send, meta_recv,
    pack_send, pack_recv, ret_send, ret_recv, fold_send, fold_recv, perm_sem,
):
    group = experts // LINE
    tokens, width = both.shape[2], both.shape[3]
    top = routes_ref.shape[0]
    section = lax.axis_index("section")
    me = lax.axis_index("expert")
    p = me // group
    q = me % group
    far = LINE - 1 - p
    part_width = width // PIECES

    def cut(piece):
        return pl.ds(piece * part_width, part_width)

    def cut_wide(piece):
        return pl.ds(piece * part_width, part_width + (LANES if piece == PIECES - 1 else 0))

    before = (section + sections - 1) % sections
    after = (section + 1) % sections

    def at(line, slot):
        return (section, line * group + slot)

    barrier = pltpu.get_barrier_semaphore()
    for step in range(1, LINE):
        pl.semaphore_signal(barrier, inc=1, device_id=at((p + step) % LINE, q), device_id_type=MESH)
    for step in range(1, group):
        pl.semaphore_signal(barrier, inc=1, device_id=at(p, (q + step) % group), device_id_type=MESH)
    for other in (before, after):
        pl.semaphore_signal(barrier, inc=1, device_id=(other, me), device_id_type=MESH)
    weights = [
        pltpu.make_async_copy(src, dst, w_sem.at[n])
        for n, (src, dst) in enumerate(((gate_ref, w_gate), (up_ref, w_up), (down_ref, w_down)))
    ]
    keep_x = pltpu.make_async_copy(x_ref, both.at[0, p], x_local)
    keep_x.start()
    pl.semaphore_wait(barrier, LINE + group)

    def own_x(way, piece):
        return pltpu.make_async_remote_copy(
            src_ref=x_ref.at[:, cut(piece)], dst_ref=both.at[0, p, :, cut(piece)],
            send_sem=own_send.at[way, piece],
            recv_sem=line_recv.at[0, p, piece], device_id=at((p + (1, LINE - 1)[way]) % LINE, q),
            device_id_type=MESH,
        )

    def line_copy(kind, origin, way, piece):
        return pltpu.make_async_remote_copy(
            src_ref=both.at[kind, origin, :, cut(piece)],
            dst_ref=both.at[kind, origin, :, cut(piece)],
            send_sem=line_send.at[kind, origin, way, piece],
            recv_sem=line_recv.at[kind, origin, piece],
            device_id=at((p + (1, LINE - 1)[way]) % LINE, q), device_id_type=MESH,
        )

    def has(way):
        return (p < LINE - 1) if way == 0 else (p > 0)

    def permute(piece):
        return pltpu.make_async_remote_copy(
            src_ref=grad_ref.at[:, cut(piece)], dst_ref=both.at[1, p, :, cut(piece)],
            send_sem=perm_sem.at[0, piece], recv_sem=perm_sem.at[1, piece],
            device_id=(before, me), device_id_type=MESH,
        )

    for piece in range(PIECES):
        for way in range(2):
            @pl.when(has(way))
            def _():
                own_x(way, piece).start()
        permute(piece).start()

    routes = routes_ref[...]
    exponent = jnp.exp(logits_ref[...])
    share = exponent / jnp.sum(exponent, axis=0, keepdims=True)
    expert_at = lax.broadcasted_iota(jnp.int32, (experts, tokens), 0)
    named = jnp.zeros((experts, tokens), F32)
    weight = jnp.zeros((experts, tokens), F32)
    for k in range(top):
        hit = routes[k:k + 1, :] == expert_at
        named = named + jnp.where(hit, 1.0, 0.0)
        weight = weight + jnp.where(hit, share[k:k + 1, :], 0.0)
    earlier = (
        lax.broadcasted_iota(jnp.int32, (tokens, tokens), 0)
        < lax.broadcasted_iota(jnp.int32, (tokens, tokens), 1)
    )
    rank = jnp.dot(
        named.astype(BF16), jnp.where(earlier, 1.0, 0.0).astype(BF16), preferred_element_type=F32
    )
    meta[p, 0] = jnp.where(named > 0.5, rank, -1.0)
    meta[p, 1] = weight

    def meta_copy(step):
        return pltpu.make_async_remote_copy(
            src_ref=meta.at[p], dst_ref=meta.at[p], send_sem=meta_send.at[step],
            recv_sem=meta_recv.at[step], device_id=at((p + step) % LINE, q), device_id_type=MESH,
        )

    def meta_wait(step):
        slot = (p + LINE - step) % LINE
        return pltpu.make_async_remote_copy(
            src_ref=meta.at[slot], dst_ref=meta.at[slot], send_sem=meta_send.at[step],
            recv_sem=meta_recv.at[step], device_id=at((p + step) % LINE, q), device_id_type=MESH,
        )

    for step in range(1, LINE):
        meta_copy(step).start()
    for copy in weights:
        copy.start()

    def chosen(origin, what, slot):
        table = meta[origin, what]
        return jnp.sum(jnp.where(expert_at == p * group + slot, table, 0.0), axis=0, keepdims=True)

    place = lax.broadcasted_iota(jnp.int32, (cap, tokens), 0).astype(F32)

    def pack_copy(kind, origin, step, piece):
        return pltpu.make_async_remote_copy(
            src_ref=pack.at[kind, origin, step - 1, :, cut(piece)],
            dst_ref=rows.at[kind, origin, q, :, cut(piece)],
            send_sem=pack_send.at[kind, origin, step, piece],
            recv_sem=pack_recv.at[kind, origin, step, piece],
            device_id=at(p, (q + step) % group), device_id_type=MESH,
        )

    def pack_wait(kind, origin, step, piece):
        return pltpu.make_async_remote_copy(
            src_ref=pack.at[kind, origin, step - 1, :, cut(piece)],
            dst_ref=rows.at[kind, origin, (q + group - step) % group, :, cut(piece)],
            send_sem=pack_send.at[kind, origin, step, piece],
            recv_sem=pack_recv.at[kind, origin, step, piece],
            device_id=at(p, (q + step) % group), device_id_type=MESH,
        )

    def do_pack(kind, origin, piece):
        source = both[kind, origin, :, cut(piece)]
        picks = [
            jnp.where(chosen(origin, 0, (q + step) % group) == place, 1.0, 0.0).astype(BF16)
            for step in range(group)
        ]
        packed = jnp.dot(
            jnp.concatenate(picks, axis=0), source, preferred_element_type=F32
        ).astype(BF16)
        for step in range(1, group):
            pack[kind, origin, step - 1, :, cut(piece)] = packed[step * cap:(step + 1) * cap]
            pack_copy(kind, origin, step, piece).start()
        rows[kind, origin, q, :, cut(piece)] = packed[:cap]

    def ret_copy(origin, step, piece):
        slot = (q + group - step) % group
        return pltpu.make_async_remote_copy(
            src_ref=ret.at[origin, slot, :, cut_wide(piece)],
            dst_ref=back.at[origin, q, :, cut_wide(piece)],
            send_sem=ret_send.at[origin, step, piece], recv_sem=ret_recv.at[origin, step, piece],
            device_id=at(p, slot), device_id_type=MESH,
        )

    def ret_wait(origin, step, piece):
        return pltpu.make_async_remote_copy(
            src_ref=ret.at[origin, (q + group - step) % group, :, cut_wide(piece)],
            dst_ref=back.at[origin, (q + step) % group, :, cut_wide(piece)],
            send_sem=ret_send.at[origin, step, piece], recv_sem=ret_recv.at[origin, step, piece],
            device_id=at(p, (q + group - step) % group), device_id_type=MESH,
        )

    def do_front(origin):
        for piece in range(PIECES):
            for step in range(1, group):
                pack_wait(0, origin, step, piece).wait_recv()
        inputs = rows[0, origin].reshape(group * cap, width)
        gate_act[origin] = jnp.dot(inputs, w_gate[...], preferred_element_type=F32).T
        up_act[origin] = jnp.dot(inputs, w_up[...], preferred_element_type=F32).T

    def do_back(origin):
        hidden = jnp.zeros((w_down.shape[0], group * cap), F32)
        for piece in range(PIECES):
            for step in range(1, group):
                pack_wait(1, origin, step, piece).wait_recv()
            grads = rows[1, origin, :, :, cut(piece)].reshape(group * cap, part_width)
            hidden = hidden + dot_nt(w_down[:, cut(piece)], grads)
        pre_gate = gate_act[origin]
        pre_up = up_act[origin]
        sigmoid = jax.nn.sigmoid(pre_gate)
        active = pre_gate * sigmoid
        up_grad = hidden * active
        dots = jnp.sum(up_grad * pre_up, axis=0, keepdims=True)
        gate_grad = hidden * pre_up * sigmoid * (1.0 + pre_gate * (1.0 - sigmoid))
        gate_grad = gate_grad.astype(BF16)
        up_grad = up_grad.astype(BF16)
        lane = lax.broadcasted_iota(jnp.int32, (LANES, group * cap), 0)
        ret[origin, :, :, width:] = (
            jnp.where(lane == me, dots, 0.0).T.astype(BF16).reshape(group, cap, LANES)
        )
        for piece in range(PIECES):
            pair = jnp.dot(w_gate[cut(piece), :], gate_grad, preferred_element_type=F32)
            pair = pair + jnp.dot(w_up[cut(piece), :], up_grad, preferred_element_type=F32)
            ret[origin, :, :, cut(piece)] = pair.T.astype(BF16).reshape(group, cap, part_width)
            for step in range(1, group):
                ret_copy(origin, step, piece).start()
        back[origin, q] = ret[origin, q]

    def fold_copy(origin, way, piece):
        target = p + 1 - 2 * way
        if way == 0:
            slot = jnp.where(origin == target, LINE, origin)
        else:
            slot = origin
        return pltpu.make_async_remote_copy(
            src_ref=fold.at[origin, :, cut_wide(piece)],
            dst_ref=fold_in.at[slot, :, cut_wide(piece)],
            send_sem=fold_send.at[origin, piece], recv_sem=fold_recv.at[slot, piece],
            device_id=at((p + (1, LINE - 1)[way]) % LINE, q), device_id_type=MESH,
        )

    def fold_wait(slot, piece):
        return pltpu.make_async_remote_copy(
            src_ref=fold.at[0, :, cut_wide(piece)], dst_ref=fold_in.at[slot, :, cut_wide(piece)],
            send_sem=fold_send.at[0, piece], recv_sem=fold_recv.at[slot, piece],
            device_id=at((p + 1) % LINE, q), device_id_type=MESH,
        )

    def do_combine(origin):
        shares = []
        for slot in range(group):
            hit = chosen(origin, 0, slot) == place
            shares.append(jnp.where(hit, chosen(origin, 1, slot), 0.0))
        weigh = jnp.concatenate(shares, axis=0).T
        high = weigh.astype(BF16)
        low = (weigh - high.astype(F32)).astype(BF16)
        pick = jnp.where(weigh > 0.0, 1.0, 0.0).astype(BF16)
        for piece in range(PIECES):
            for step in range(1, group):
                ret_wait(origin, step, piece).wait_recv()
            came = back[origin, :, :, cut(piece)].reshape(group * cap, part_width)
            part[origin, :, cut(piece)] = (
                jnp.dot(high, came, preferred_element_type=F32)
                + jnp.dot(low, came, preferred_element_type=F32)
            )
            if piece == PIECES - 1:
                marks = back[origin, :, :, width:].reshape(group * cap, LANES)
                part[origin, :, width:] = jnp.dot(pick, marks, preferred_element_type=F32)

            @pl.when((p == LINE - 1) & (origin < p))
            def _():
                fold[origin, :, cut_wide(piece)] = part[origin, :, cut_wide(piece)].astype(BF16)
                fold_copy(origin, 1, piece).start()

            @pl.when((p == 0) & (origin > p))
            def _():
                fold[origin, :, cut_wide(piece)] = part[origin, :, cut_wide(piece)].astype(BF16)
                fold_copy(origin, 0, piece).start()

    keep_x.wait()
    for piece in range(PIECES):
        do_pack(0, p, piece)
    for copy in weights:
        copy.wait()
    do_front(p)
    for step in range(1, LINE):
        meta_wait(step).wait_recv()

    def arrival(way, i):
        count = p if way == 0 else far
        kind = jnp.where(i >= count, 1, 0)
        if way == 0:
            origin = jnp.where(i >= count, i - count, p - 1 - i)
        else:
            origin = jnp.where(i >= count, LINE - 1 - (i - count), p + 1 + i)
        valid = (i >= 0) & (i < 2 * count)
        return valid, kind, jnp.clip(origin, 0, LINE - 1)

    def candidate(n, i):
        valid_up, kind_up, origin_up = arrival(0, i)
        valid_down, kind_down, origin_down = arrival(1, i)
        valid = jnp.where(n == 0, jnp.where(i == 0, 1, 0), jnp.where(
            n == 1, jnp.where(valid_up, 1, 0), jnp.where(valid_down, 1, 0)))
        kind = jnp.where(n == 0, 1, jnp.where(n == 1, kind_up, kind_down))
        origin = jnp.where(n == 0, p, jnp.where(n == 1, origin_up, origin_down))
        return valid == 1, kind, origin

    late = jnp.where((p == 0) | (p == LINE - 1), 0, 1)

    def turn(i, carry):
        def forward(piece):
            @pl.when(i == 0)
            def _():
                permute(piece).wait_recv()

            for way in range(2):
                valid, kind, origin = arrival(way, i)

                @pl.when(valid)
                def _():
                    line_copy(kind, origin, way, piece).wait_recv()

                    @pl.when(has(way))
                    def _():
                        line_copy(kind, origin, way, piece).start()

        def own_gradients():
            for way in range(2):
                count = p if way == 0 else far

                @pl.when((i == jnp.maximum(2 * count - 1, 0)) & has(way))
                def _():
                    for piece in range(PIECES):
                        line_copy(1, p, way, piece).start()

        def each(step, body, own_step=None):
            def one(n, carry):
                valid, kind, origin = candidate(
                    n, step if own_step is None else jnp.where(n == 0, own_step, step)
                )
                body(valid, kind, origin)
                return carry

            lax.fori_loop(0, 3, one, 0)

        def pack_one(piece, valid, kind, origin):
            @pl.when(valid)
            def _():
                do_pack(kind, origin, piece)

        def combine_one(valid, kind, origin):
            @pl.when(valid & (kind == 1))
            def _():
                do_combine(origin)

        def front_one(valid, kind, origin):
            @pl.when(valid & (kind == 0))
            def _():
                do_front(origin)

        def back_one(valid, kind, origin):
            @pl.when(valid & (kind == 1))
            def _():
                do_back(origin)

        for piece in range(PIECES):
            forward(piece)
            if piece == PIECES - 1:
                own_gradients()
            each(i, functools.partial(pack_one, piece))
            if piece == 0:
                each(i - 1, front_one)

                @pl.when(late == 0)
                def _():
                    each(i - 1, combine_one)

        each(i - late, back_one, i)

        @pl.when(late == 1)
        def _():
            each(i - 2, combine_one)

        return carry

    lax.fori_loop(0, 2 * LINE - 1, turn, 0)

    def gather_back(r, carry):
        origin = LINE - 1 - r
        for piece in range(PIECES):
            where = cut_wide(piece)

            @pl.when((p < LINE - 1) & (r < p))
            def _():
                fold_wait(r, piece).wait_recv()
                summed = part[r, :, where] + fold_in[r, :, where].astype(F32)
                fold[r, :, where] = summed.astype(BF16)
                fold_copy(r, 1, piece).start()

            @pl.when((p > 0) & (origin > p))
            def _():
                fold_wait(origin, piece).wait_recv()
                summed = part[origin, :, where] + fold_in[origin, :, where].astype(F32)
                fold[origin, :, where] = summed.astype(BF16)
                fold_copy(origin, 0, piece).start()

        return carry

    lax.fori_loop(0, LINE - 1, gather_back, 0)
    for piece in range(PIECES):
        where = cut_wide(piece)
        for way in range(2):
            @pl.when(has(1 - way))
            def _():
                slot = LINE if way == 0 else p
                fold_wait(slot, piece).wait_recv()
                part[p, :, where] = part[p, :, where] + fold_in[slot, :, where].astype(F32)

    total_ref[...] = part[p, :, :width] + both[1, p].astype(F32)
    dots_ref[...] = part[p, :, width:]

    for step in range(1, LINE):
        meta_copy(step).wait_send()
    for piece in range(PIECES):
        permute(piece).wait_send()
        for way in range(2):
            @pl.when(has(way))
            def _():
                own_x(way, piece).wait_send()
                line_copy(1, p, way, piece).wait_send()

    def finish(origin, carry):
        for piece in range(PIECES):
            for kind in range(2):
                for step in range(1, group):
                    pack_copy(kind, origin, step, piece).wait_send()

                @pl.when((origin < p) & has(0))
                def _():
                    line_copy(kind, origin, 0, piece).wait_send()

                @pl.when((origin > p) & has(1))
                def _():
                    line_copy(kind, origin, 1, piece).wait_send()

            for step in range(1, group):
                ret_copy(origin, step, piece).wait_send()

            @pl.when(origin < p)
            def _():
                fold_copy(origin, 1, piece).wait_send()

            @pl.when(origin > p)
            def _():
                fold_copy(origin, 0, piece).wait_send()

        return carry

    lax.fori_loop(0, LINE, finish, 0)


def exchange(sections, x, grad, routes, logits, w_gate, w_up, w_down, capacity):
    tokens, width = x.shape
    hidden = w_gate.shape[1]
    experts = lax.axis_size("expert")
    group = experts // LINE
    cap = -(-capacity // 16) * 16
    wide = width + LANES
    vmem = pl.BlockSpec(memory_space=pltpu.VMEM)
    anywhere = pl.BlockSpec(memory_space=pl.ANY)
    dma = pltpu.SemaphoreType.DMA
    flops = 2 * LINE * group * cap * width * hidden * 5
    return pl.pallas_call(
        functools.partial(kernel, sections, experts, cap),
        out_shape=(
            jax.ShapeDtypeStruct((tokens, width), F32),
            jax.ShapeDtypeStruct((tokens, LANES), F32),
        ),
        in_specs=[anywhere, anywhere, vmem, vmem, anywhere, anywhere, anywhere],
        out_specs=(vmem, vmem),
        scratch_shapes=[
            pltpu.VMEM((2, LINE, tokens, width), BF16),
            pltpu.VMEM((2, LINE, group - 1, cap, width), BF16),
            pltpu.VMEM((2, LINE, group, cap, width), BF16),
            pltpu.VMEM((LINE, group, cap, wide), BF16),
            pltpu.VMEM((LINE, group, cap, wide), BF16),
            pltpu.VMEM((LINE, tokens, wide), F32),
            pltpu.VMEM((LINE, tokens, wide), BF16),
            pltpu.VMEM((LINE + 1, tokens, wide), BF16),
            pltpu.VMEM((LINE, 2, experts, tokens), F32),
            pltpu.VMEM((LINE, hidden, group * cap), F32),
            pltpu.VMEM((LINE, hidden, group * cap), F32),
            pltpu.VMEM((width, hidden), BF16),
            pltpu.VMEM((width, hidden), BF16),
            pltpu.VMEM((hidden, width), BF16),
            dma(()),
            dma((3,)),
            dma((2, PIECES)),
            dma((2, LINE, 2, PIECES)),
            dma((2, LINE, PIECES)),
            dma((LINE,)),
            dma((LINE,)),
            dma((2, LINE, group, PIECES)),
            dma((2, LINE, group, PIECES)),
            dma((LINE, group, PIECES)),
            dma((LINE, group, PIECES)),
            dma((LINE, PIECES)),
            dma((LINE + 1, PIECES)),
            dma((2, PIECES)),
        ],
        compiler_params=pltpu.CompilerParams(
            collective_id=0, has_side_effects=True, vmem_limit_bytes=63 * 1024 * 1024
        ),
        cost_estimate=pl.CostEstimate(
            flops=flops, bytes_accessed=2 * 3 * width * hidden, transcendentals=0
        ),
    )(x, grad, routes, logits, w_gate, w_up, w_down)


def per_device(
    grad_out, layer_input, routes, route_logits, gate_weight, up_weight, down_weight, router_weight
):
    token_count = layer_input.shape[1]
    top_count = routes.shape[2]
    every_expert = router_weight.shape[2]
    capacity = 2 * token_count * top_count // every_expert
    w_router = router_weight[0]
    picks = routes[0]
    total, dots = exchange(
        lax.axis_size("section"), layer_input[0], grad_out[0], picks.T, route_logits[0].T,
        gate_weight[0, 0], up_weight[0, 0], down_weight[0, 0], capacity,
    )
    exponent = jnp.exp(route_logits[0])
    route_weight = exponent / jnp.sum(exponent, axis=1, keepdims=True)
    lane = jnp.arange(LANES, dtype=jnp.int32)[None, None, :]
    weight_grad = jnp.sum(jnp.where(picks[:, :, None] == lane, dots[:, None, :], 0.0), axis=2)
    center = jnp.sum(route_weight * weight_grad, axis=1, keepdims=True)
    logit_grad = route_weight * (weight_grad - center)
    matches = picks[:, :, None] == jnp.arange(every_expert, dtype=jnp.int32)[None, None, :]
    dense_grad = jnp.sum(jnp.where(matches, logit_grad[:, :, None], 0.0), axis=1)
    router_grad = jnp.dot(
        dense_grad, w_router.astype(jnp.float32).T, precision=lax.Precision.HIGHEST
    )
    grad_in = (total + router_grad).astype(jnp.bfloat16)
    return (grad_in[None], logit_grad[None])


def solution(mesh):
    in_specs = (
        P("section", "expert", None),
        P("section", "expert", None),
        P("section", "expert", None),
        P("section", "expert", None),
        P("section", "expert", None, None),
        P("section", "expert", None, None),
        P("section", "expert", None, None),
        P("section", None, None),
    )
    out_specs = (P("section", "expert", None), P("section", "expert", None))
    return jax.shard_map(
        per_device, mesh=mesh, in_specs=in_specs, out_specs=out_specs, check_vma=False
    )
```

```python
import functools

import jax
import jax.numpy as jnp
from jax import lax
from jax.experimental import pallas as pl
from jax.experimental.pallas import tpu as pltpu
from jax.sharding import PartitionSpec as P

MESH = pl.DeviceIdType.MESH
LINE = 4
LANES = 128
PIECES = 2
F32 = jnp.float32
BF16 = jnp.bfloat16


def dot_nt(a, b):
    return lax.dot_general(a, b, (((1,), (1,)), ((), ())), preferred_element_type=F32)


def kernel(
    sections, experts, cap,
    x_ref, grad_ref, routes_ref, logits_ref, gate_ref, up_ref, down_ref,
    total_ref, dots_ref,
    both, pack, rows, ret, back, part, fold, fold_in, meta, gate_act, up_act, w_gate, w_up, w_down,
    x_local, w_sem, own_send, line_send, line_recv, meta_send, meta_recv,
    pack_send, pack_recv, ret_send, ret_recv, fold_send, fold_recv, perm_sem,
):
    group = experts // LINE
    tokens, width = both.shape[2], both.shape[3]
    top = routes_ref.shape[0]
    section = lax.axis_index("section")
    me = lax.axis_index("expert")
    p = me // group
    q = me % group
    far = LINE - 1 - p
    part_width = width // PIECES

    def cut(piece):
        return pl.ds(piece * part_width, part_width)

    def cut_wide(piece):
        return pl.ds(piece * part_width, part_width + (LANES if piece == PIECES - 1 else 0))

    before = (section + sections - 1) % sections
    after = (section + 1) % sections

    def at(line, slot):
        return (section, line * group + slot)

    barrier = pltpu.get_barrier_semaphore()
    for step in range(1, LINE):
        pl.semaphore_signal(barrier, inc=1, device_id=at((p + step) % LINE, q), device_id_type=MESH)
    for step in range(1, group):
        pl.semaphore_signal(barrier, inc=1, device_id=at(p, (q + step) % group), device_id_type=MESH)
    for other in (before, after):
        pl.semaphore_signal(barrier, inc=1, device_id=(other, me), device_id_type=MESH)
    weights = [
        pltpu.make_async_copy(src, dst, w_sem.at[n])
        for n, (src, dst) in enumerate(((gate_ref, w_gate), (up_ref, w_up), (down_ref, w_down)))
    ]
    keep_x = pltpu.make_async_copy(x_ref, both.at[0, p], x_local)
    keep_x.start()
    pl.semaphore_wait(barrier, LINE + group)

    def own_x(way, piece):
        return pltpu.make_async_remote_copy(
            src_ref=x_ref.at[:, cut(piece)], dst_ref=both.at[0, p, :, cut(piece)],
            send_sem=own_send.at[way, piece],
            recv_sem=line_recv.at[0, p, piece], device_id=at((p + (1, LINE - 1)[way]) % LINE, q),
            device_id_type=MESH,
        )

    def line_copy(kind, origin, way, piece):
        return pltpu.make_async_remote_copy(
            src_ref=both.at[kind, origin, :, cut(piece)],
            dst_ref=both.at[kind, origin, :, cut(piece)],
            send_sem=line_send.at[kind, origin, way, piece],
            recv_sem=line_recv.at[kind, origin, piece],
            device_id=at((p + (1, LINE - 1)[way]) % LINE, q), device_id_type=MESH,
        )

    def has(way):
        return (p < LINE - 1) if way == 0 else (p > 0)

    def permute(piece):
        return pltpu.make_async_remote_copy(
            src_ref=grad_ref.at[:, cut(piece)], dst_ref=both.at[1, p, :, cut(piece)],
            send_sem=perm_sem.at[0, piece], recv_sem=perm_sem.at[1, piece],
            device_id=(before, me), device_id_type=MESH,
        )

    for piece in range(PIECES):
        for way in range(2):
            @pl.when(has(way))
            def _():
                own_x(way, piece).start()
        permute(piece).start()

    routes = routes_ref[...]
    exponent = jnp.exp(logits_ref[...])
    share = exponent / jnp.sum(exponent, axis=0, keepdims=True)
    expert_at = lax.broadcasted_iota(jnp.int32, (experts, tokens), 0)
    named = jnp.zeros((experts, tokens), F32)
    weight = jnp.zeros((experts, tokens), F32)
    for k in range(top):
        hit = routes[k:k + 1, :] == expert_at
        named = named + jnp.where(hit, 1.0, 0.0)
        weight = weight + jnp.where(hit, share[k:k + 1, :], 0.0)
    earlier = (
        lax.broadcasted_iota(jnp.int32, (tokens, tokens), 0)
        < lax.broadcasted_iota(jnp.int32, (tokens, tokens), 1)
    )
    rank = jnp.dot(
        named.astype(BF16), jnp.where(earlier, 1.0, 0.0).astype(BF16), preferred_element_type=F32
    )
    meta[p, 0] = jnp.where(named > 0.5, rank, -1.0)
    meta[p, 1] = weight

    def meta_copy(step):
        return pltpu.make_async_remote_copy(
            src_ref=meta.at[p], dst_ref=meta.at[p], send_sem=meta_send.at[step],
            recv_sem=meta_recv.at[step], device_id=at((p + step) % LINE, q), device_id_type=MESH,
        )

    def meta_wait(step):
        slot = (p + LINE - step) % LINE
        return pltpu.make_async_remote_copy(
            src_ref=meta.at[slot], dst_ref=meta.at[slot], send_sem=meta_send.at[step],
            recv_sem=meta_recv.at[step], device_id=at((p + step) % LINE, q), device_id_type=MESH,
        )

    for step in range(1, LINE):
        meta_copy(step).start()
    for copy in weights:
        copy.start()

    def chosen(origin, what, slot):
        table = meta[origin, what]
        return jnp.sum(jnp.where(expert_at == p * group + slot, table, 0.0), axis=0, keepdims=True)

    place = lax.broadcasted_iota(jnp.int32, (cap, tokens), 0).astype(F32)

    def pack_copy(kind, origin, step, piece):
        return pltpu.make_async_remote_copy(
            src_ref=pack.at[kind, origin, step - 1, :, cut(piece)],
            dst_ref=rows.at[kind, origin, q, :, cut(piece)],
            send_sem=pack_send.at[kind, origin, step, piece],
            recv_sem=pack_recv.at[kind, origin, step, piece],
            device_id=at(p, (q + step) % group), device_id_type=MESH,
        )

    def pack_wait(kind, origin, step, piece):
        return pltpu.make_async_remote_copy(
            src_ref=pack.at[kind, origin, step - 1, :, cut(piece)],
            dst_ref=rows.at[kind, origin, (q + group - step) % group, :, cut(piece)],
            send_sem=pack_send.at[kind, origin, step, piece],
            recv_sem=pack_recv.at[kind, origin, step, piece],
            device_id=at(p, (q + step) % group), device_id_type=MESH,
        )

    def do_pack(kind, origin, piece):
        source = both[kind, origin, :, cut(piece)]
        picks = [
            jnp.where(chosen(origin, 0, (q + step) % group) == place, 1.0, 0.0).astype(BF16)
            for step in range(group)
        ]
        packed = jnp.dot(
            jnp.concatenate(picks, axis=0), source, preferred_element_type=F32
        ).astype(BF16)
        for step in range(1, group):
            pack[kind, origin, step - 1, :, cut(piece)] = packed[step * cap:(step + 1) * cap]
            pack_copy(kind, origin, step, piece).start()
        rows[kind, origin, q, :, cut(piece)] = packed[:cap]

    def ret_copy(origin, step, piece):
        slot = (q + group - step) % group
        return pltpu.make_async_remote_copy(
            src_ref=ret.at[origin, slot, :, cut_wide(piece)],
            dst_ref=back.at[origin, q, :, cut_wide(piece)],
            send_sem=ret_send.at[origin, step, piece], recv_sem=ret_recv.at[origin, step, piece],
            device_id=at(p, slot), device_id_type=MESH,
        )

    def ret_wait(origin, step, piece):
        return pltpu.make_async_remote_copy(
            src_ref=ret.at[origin, (q + group - step) % group, :, cut_wide(piece)],
            dst_ref=back.at[origin, (q + step) % group, :, cut_wide(piece)],
            send_sem=ret_send.at[origin, step, piece], recv_sem=ret_recv.at[origin, step, piece],
            device_id=at(p, (q + group - step) % group), device_id_type=MESH,
        )

    def do_front(origin):
        for piece in range(PIECES):
            for step in range(1, group):
                pack_wait(0, origin, step, piece).wait_recv()
        inputs = rows[0, origin].reshape(group * cap, width)
        gate_act[origin] = jnp.dot(inputs, w_gate[...], preferred_element_type=F32).T
        up_act[origin] = jnp.dot(inputs, w_up[...], preferred_element_type=F32).T

    def do_back(origin):
        hidden = jnp.zeros((w_down.shape[0], group * cap), F32)
        for piece in range(PIECES):
            for step in range(1, group):
                pack_wait(1, origin, step, piece).wait_recv()
            grads = rows[1, origin, :, :, cut(piece)].reshape(group * cap, part_width)
            hidden = hidden + dot_nt(w_down[:, cut(piece)], grads)
        pre_gate = gate_act[origin]
        pre_up = up_act[origin]
        sigmoid = jax.nn.sigmoid(pre_gate)
        active = pre_gate * sigmoid
        up_grad = hidden * active
        dots = jnp.sum(up_grad * pre_up, axis=0, keepdims=True)
        gate_grad = hidden * pre_up * sigmoid * (1.0 + pre_gate * (1.0 - sigmoid))
        gate_grad = gate_grad.astype(BF16)
        up_grad = up_grad.astype(BF16)
        lane = lax.broadcasted_iota(jnp.int32, (LANES, group * cap), 0)
        ret[origin, :, :, width:] = (
            jnp.where(lane == me, dots, 0.0).T.astype(BF16).reshape(group, cap, LANES)
        )
        for piece in range(PIECES):
            pair = jnp.dot(w_gate[cut(piece), :], gate_grad, preferred_element_type=F32)
            pair = pair + jnp.dot(w_up[cut(piece), :], up_grad, preferred_element_type=F32)
            ret[origin, :, :, cut(piece)] = pair.T.astype(BF16).reshape(group, cap, part_width)
            for step in range(1, group):
                ret_copy(origin, step, piece).start()
        back[origin, q] = ret[origin, q]

    def fold_copy(origin, way, piece):
        target = p + 1 - 2 * way
        if way == 0:
            slot = jnp.where(origin == target, LINE, origin)
        else:
            slot = origin
        return pltpu.make_async_remote_copy(
            src_ref=fold.at[origin, :, cut_wide(piece)],
            dst_ref=fold_in.at[slot, :, cut_wide(piece)],
            send_sem=fold_send.at[origin, piece], recv_sem=fold_recv.at[slot, piece],
            device_id=at((p + (1, LINE - 1)[way]) % LINE, q), device_id_type=MESH,
        )

    def fold_wait(slot, piece):
        return pltpu.make_async_remote_copy(
            src_ref=fold.at[0, :, cut_wide(piece)], dst_ref=fold_in.at[slot, :, cut_wide(piece)],
            send_sem=fold_send.at[0, piece], recv_sem=fold_recv.at[slot, piece],
            device_id=at((p + 1) % LINE, q), device_id_type=MESH,
        )

    def do_combine(origin):
        shares = []
        for slot in range(group):
            hit = chosen(origin, 0, slot) == place
            shares.append(jnp.where(hit, chosen(origin, 1, slot), 0.0))
        weigh = jnp.concatenate(shares, axis=0).T
        high = weigh.astype(BF16)
        low = (weigh - high.astype(F32)).astype(BF16)
        pick = jnp.where(weigh > 0.0, 1.0, 0.0).astype(BF16)
        for piece in range(PIECES):
            for step in range(1, group):
                ret_wait(origin, step, piece).wait_recv()
            came = back[origin, :, :, cut(piece)].reshape(group * cap, part_width)
            part[origin, :, cut(piece)] = (
                jnp.dot(high, came, preferred_element_type=F32)
                + jnp.dot(low, came, preferred_element_type=F32)
            )
            if piece == PIECES - 1:
                marks = back[origin, :, :, width:].reshape(group * cap, LANES)
                part[origin, :, width:] = jnp.dot(pick, marks, preferred_element_type=F32)

            @pl.when((p == LINE - 1) & (origin < p))
            def _():
                fold[origin, :, cut_wide(piece)] = part[origin, :, cut_wide(piece)].astype(BF16)
                fold_copy(origin, 1, piece).start()

            @pl.when((p == 0) & (origin > p))
            def _():
                fold[origin, :, cut_wide(piece)] = part[origin, :, cut_wide(piece)].astype(BF16)
                fold_copy(origin, 0, piece).start()

    keep_x.wait()
    for piece in range(PIECES):
        do_pack(0, p, piece)
    for copy in weights:
        copy.wait()
    do_front(p)
    for step in range(1, LINE):
        meta_wait(step).wait_recv()

    def arrival(way, i):
        count = p if way == 0 else far
        kind = jnp.where(i >= count, 1, 0)
        if way == 0:
            origin = jnp.where(i >= count, i - count, p - 1 - i)
        else:
            origin = jnp.where(i >= count, LINE - 1 - (i - count), p + 1 + i)
        valid = (i >= 0) & (i < 2 * count)
        return valid, kind, jnp.clip(origin, 0, LINE - 1)

    def candidate(n, i):
        valid_up, kind_up, origin_up = arrival(0, i)
        valid_down, kind_down, origin_down = arrival(1, i)
        valid = jnp.where(n == 0, jnp.where(i == 0, 1, 0), jnp.where(
            n == 1, jnp.where(valid_up, 1, 0), jnp.where(valid_down, 1, 0)))
        kind = jnp.where(n == 0, 1, jnp.where(n == 1, kind_up, kind_down))
        origin = jnp.where(n == 0, p, jnp.where(n == 1, origin_up, origin_down))
        return valid == 1, kind, origin

    late = jnp.where((p == 0) | (p == LINE - 1), 0, 1)

    def turn(i, carry):
        def forward(piece):
            @pl.when(i == 0)
            def _():
                permute(piece).wait_recv()

            for way in range(2):
                valid, kind, origin = arrival(way, i)

                @pl.when(valid)
                def _():
                    line_copy(kind, origin, way, piece).wait_recv()

                    @pl.when(has(way))
                    def _():
                        line_copy(kind, origin, way, piece).start()

        def own_gradients():
            for way in range(2):
                count = p if way == 0 else far

                @pl.when((i == jnp.maximum(2 * count - 1, 0)) & has(way))
                def _():
                    for piece in range(PIECES):
                        line_copy(1, p, way, piece).start()

        def each(step, body):
            def one(n, carry):
                valid, kind, origin = candidate(n, step)
                body(valid, kind, origin)
                return carry

            lax.fori_loop(0, 3, one, 0)

        def pack_one(piece, valid, kind, origin):
            @pl.when(valid)
            def _():
                do_pack(kind, origin, piece)

        def combine_one(valid, kind, origin):
            @pl.when(valid & (kind == 1))
            def _():
                do_combine(origin)

        def front_one(valid, kind, origin):
            @pl.when(valid & (kind == 0))
            def _():
                do_front(origin)

        def back_one(valid, kind, origin):
            @pl.when(valid & (kind == 1))
            def _():
                do_back(origin)

        for piece in range(PIECES):
            forward(piece)
            if piece == PIECES - 1:
                own_gradients()
            each(i, functools.partial(pack_one, piece))
            if piece == 0:
                each(i - 1, front_one)

                @pl.when(late == 0)
                def _():
                    each(i - 1, combine_one)

        each(i - late, back_one)

        @pl.when(late == 1)
        def _():
            each(i - 2, combine_one)

        return carry

    lax.fori_loop(0, 2 * LINE - 1, turn, 0)

    def gather_back(r, carry):
        origin = LINE - 1 - r
        for piece in range(PIECES):
            where = cut_wide(piece)

            @pl.when((p < LINE - 1) & (r < p))
            def _():
                fold_wait(r, piece).wait_recv()
                summed = part[r, :, where] + fold_in[r, :, where].astype(F32)
                fold[r, :, where] = summed.astype(BF16)
                fold_copy(r, 1, piece).start()

            @pl.when((p > 0) & (origin > p))
            def _():
                fold_wait(origin, piece).wait_recv()
                summed = part[origin, :, where] + fold_in[origin, :, where].astype(F32)
                fold[origin, :, where] = summed.astype(BF16)
                fold_copy(origin, 0, piece).start()

        return carry

    lax.fori_loop(0, LINE - 1, gather_back, 0)
    for piece in range(PIECES):
        where = cut_wide(piece)
        for way in range(2):
            @pl.when(has(1 - way))
            def _():
                slot = LINE if way == 0 else p
                fold_wait(slot, piece).wait_recv()
                part[p, :, where] = part[p, :, where] + fold_in[slot, :, where].astype(F32)

    total_ref[...] = part[p, :, :width] + both[1, p].astype(F32)
    dots_ref[...] = part[p, :, width:]

    for step in range(1, LINE):
        meta_copy(step).wait_send()
    for piece in range(PIECES):
        permute(piece).wait_send()
        for way in range(2):
            @pl.when(has(way))
            def _():
                own_x(way, piece).wait_send()
                line_copy(1, p, way, piece).wait_send()

    def finish(origin, carry):
        for piece in range(PIECES):
            for kind in range(2):
                for step in range(1, group):
                    pack_copy(kind, origin, step, piece).wait_send()

                @pl.when((origin < p) & has(0))
                def _():
                    line_copy(kind, origin, 0, piece).wait_send()

                @pl.when((origin > p) & has(1))
                def _():
                    line_copy(kind, origin, 1, piece).wait_send()

            for step in range(1, group):
                ret_copy(origin, step, piece).wait_send()

            @pl.when(origin < p)
            def _():
                fold_copy(origin, 1, piece).wait_send()

            @pl.when(origin > p)
            def _():
                fold_copy(origin, 0, piece).wait_send()

        return carry

    lax.fori_loop(0, LINE, finish, 0)


def exchange(sections, x, grad, routes, logits, w_gate, w_up, w_down, capacity):
    tokens, width = x.shape
    hidden = w_gate.shape[1]
    experts = lax.axis_size("expert")
    group = experts // LINE
    cap = -(-capacity // 16) * 16
    wide = width + LANES
    vmem = pl.BlockSpec(memory_space=pltpu.VMEM)
    anywhere = pl.BlockSpec(memory_space=pl.ANY)
    dma = pltpu.SemaphoreType.DMA
    flops = 2 * LINE * group * cap * width * hidden * 5
    return pl.pallas_call(
        functools.partial(kernel, sections, experts, cap),
        out_shape=(
            jax.ShapeDtypeStruct((tokens, width), F32),
            jax.ShapeDtypeStruct((tokens, LANES), F32),
        ),
        in_specs=[anywhere, anywhere, vmem, vmem, anywhere, anywhere, anywhere],
        out_specs=(vmem, vmem),
        scratch_shapes=[
            pltpu.VMEM((2, LINE, tokens, width), BF16),
            pltpu.VMEM((2, LINE, group - 1, cap, width), BF16),
            pltpu.VMEM((2, LINE, group, cap, width), BF16),
            pltpu.VMEM((LINE, group, cap, wide), BF16),
            pltpu.VMEM((LINE, group, cap, wide), BF16),
            pltpu.VMEM((LINE, tokens, wide), F32),
            pltpu.VMEM((LINE, tokens, wide), BF16),
            pltpu.VMEM((LINE + 1, tokens, wide), BF16),
            pltpu.VMEM((LINE, 2, experts, tokens), F32),
            pltpu.VMEM((LINE, hidden, group * cap), F32),
            pltpu.VMEM((LINE, hidden, group * cap), F32),
            pltpu.VMEM((width, hidden), BF16),
            pltpu.VMEM((width, hidden), BF16),
            pltpu.VMEM((hidden, width), BF16),
            dma(()),
            dma((3,)),
            dma((2, PIECES)),
            dma((2, LINE, 2, PIECES)),
            dma((2, LINE, PIECES)),
            dma((LINE,)),
            dma((LINE,)),
            dma((2, LINE, group, PIECES)),
            dma((2, LINE, group, PIECES)),
            dma((LINE, group, PIECES)),
            dma((LINE, group, PIECES)),
            dma((LINE, PIECES)),
            dma((LINE + 1, PIECES)),
            dma((2, PIECES)),
        ],
        compiler_params=pltpu.CompilerParams(
            collective_id=0, has_side_effects=True, vmem_limit_bytes=63 * 1024 * 1024
        ),
        cost_estimate=pl.CostEstimate(
            flops=flops, bytes_accessed=2 * 3 * width * hidden, transcendentals=0
        ),
    )(x, grad, routes, logits, w_gate, w_up, w_down)


def per_device(
    grad_out, layer_input, routes, route_logits, gate_weight, up_weight, down_weight, router_weight
):
    token_count = layer_input.shape[1]
    top_count = routes.shape[2]
    every_expert = router_weight.shape[2]
    capacity = 2 * token_count * top_count // every_expert
    w_router = router_weight[0]
    picks = routes[0]
    total, dots = exchange(
        lax.axis_size("section"), layer_input[0], grad_out[0], picks.T, route_logits[0].T,
        gate_weight[0, 0], up_weight[0, 0], down_weight[0, 0], capacity,
    )
    exponent = jnp.exp(route_logits[0])
    route_weight = exponent / jnp.sum(exponent, axis=1, keepdims=True)
    lane = jnp.arange(LANES, dtype=jnp.int32)[None, None, :]
    weight_grad = jnp.sum(jnp.where(picks[:, :, None] == lane, dots[:, None, :], 0.0), axis=2)
    center = jnp.sum(route_weight * weight_grad, axis=1, keepdims=True)
    logit_grad = route_weight * (weight_grad - center)
    matches = picks[:, :, None] == jnp.arange(every_expert, dtype=jnp.int32)[None, None, :]
    dense_grad = jnp.sum(jnp.where(matches, logit_grad[:, :, None], 0.0), axis=1)
    router_grad = jnp.dot(
        dense_grad, w_router.astype(jnp.float32).T, precision=lax.Precision.HIGHEST
    )
    grad_in = (total + router_grad).astype(jnp.bfloat16)
    return (grad_in[None], logit_grad[None])


def solution(mesh):
    in_specs = (
        P("section", "expert", None),
        P("section", "expert", None),
        P("section", "expert", None),
        P("section", "expert", None),
        P("section", "expert", None, None),
        P("section", "expert", None, None),
        P("section", "expert", None, None),
        P("section", None, None),
    )
    out_specs = (P("section", "expert", None), P("section", "expert", None))
    return jax.shard_map(
        per_device, mesh=mesh, in_specs=in_specs, out_specs=out_specs, check_vma=False
    )
```
